32 devices in a mesh: seq: 4 (over y, x), zero: 8 (over z, core).
Axes of the slice: x: 2, y: 2, z: 4, core: 2. Of those that a mesh axis runs over, the one named last changes fastest.
Arguments:
- q_proj: bfloat16 [8, 1024, 2560], P('zero', 'seq'), as said below
- k_proj: bfloat16 [8, 1024, 2560], P('zero', 'seq'), as said below
- v_proj: bfloat16 [8, 1024, 2560], P('zero', 'seq'), may hold values from -6 to 6
- neighbours: int32 [8, 8, 4], P('zero'), may hold values from 0 to 7, as said below
- counts: int32 [8, 8], P('zero'), may hold values from 1 to 4
- w_out: bfloat16 [2560, 5120], P(('seq', 'zero')), may hold values from -0.125 to 0.125
- d_out: bfloat16 [8, 1024, 5120], P('zero', 'seq'), may hold values from -6 to 6
Outputs:
- out_y: bfloat16 [8, 1024, 5120], P('zero', 'seq')
- grad_q: bfloat16 [8, 1024, 2560], P('zero', 'seq')
- grad_k: bfloat16 [8, 1024, 2560], P('zero', 'seq')
- grad_v: bfloat16 [8, 1024, 2560], P('zero', 'seq')
- grad_w: float32 [2560, 5120], P(('seq', 'zero'))
The draws below stay inside these ranges and needn't reach their ends.
Inputs may be any that keep to these rules, and one draw needn't show every extreme that they name: Entries of q_proj lie within -16 and 16. Entries of k_proj lie within -16 and 16. `neighbours`: for each clip and block the 4 entries are distinct block numbers of that clip, the first being the block itself.
All inputs are finite; a program needn't handle non-finite values.
Results may differ from the reference program's by a relative error of at most 0.018.
Values may be sent and summed in bfloat16 or wider, within the bound.
No kernel may reach another device: no remote copies, remote signals or barrier semaphores. Data moves between devices by JAX's collectives and lax.ppermute only.
A program may use at most 192 MiB of HBM per device.

```python
import math
import jax
import jax.numpy as jnp
from jax import lax

D = 5120
HEADS = 20
HD = 128
BLK = 128
NB = 8
MAXN = 4
CT = 1024
CLIPS = 8
N_SEQ = 4


def paired_draw(key):
    shape = (CLIPS, NB * BLK, HEADS * HD)
    keys_part = jnp.clip(jax.random.normal(jax.random.fold_in(key, 11), shape, jnp.float32), -3.0, 3.0)
    query_part = jnp.clip(jax.random.normal(jax.random.fold_in(key, 12), shape, jnp.float32), -3.0, 3.0)
    return (query_part, keys_part)


def draw_q_proj(key, part):
    return paired_draw(key)[0].astype(jnp.bfloat16)


def draw_k_proj(key, part):
    return paired_draw(key)[1].astype(jnp.bfloat16)


def draw_neighbours(key, part):
    total_rows = CLIPS * NB
    row_keys = jax.random.split(jax.random.fold_in(key, 21), total_rows)
    shuffled = jax.vmap(lambda row_key: jax.random.permutation(row_key, NB))(row_keys)
    own_block = jnp.arange(total_rows) % NB
    columns = jnp.arange(NB)
    ranking = jnp.where(columns[None, :] == own_block[:, None], -1, shuffled)
    order = jnp.argsort(ranking, axis=1, stable=True)
    return order[:, :MAXN].reshape(CLIPS, NB, MAXN).astype(jnp.int32)


def draw_counts(key, part):
    drawn = jax.random.randint(jax.random.fold_in(key, 31), (CLIPS, NB), 1, MAXN + 1)
    drawn = drawn.at[0, 0].set(MAXN)
    drawn = drawn.at[0, 1].set(1)
    return drawn.astype(jnp.int32)


def steps_of(own_key, dims, shards, smallest, top_value):
    def one(dim, blocks):
        steps = jax.random.uniform(jax.random.fold_in(jax.random.fold_in(own_key, 6), dim), (blocks,), jnp.float32, smallest / len(shards), top_value / len(shards))
        return jnp.repeat(jnp.exp(steps), dims[dim] // blocks).reshape((-1,) + (1,) * (len(dims) - dim - 1))

    gain = one(*shards[0])
    for cut in shards[1:]:
        gain = gain * one(*cut)
    return gain


def scatter_about(key, dims, deviation, bound, cuts=(), kind=jnp.bfloat16):
    entries = deviation * jax.random.normal(key, dims, jnp.float32)
    if cuts:
        entries = entries * steps_of(key, dims, cuts, -0.22, 0.18)
    return jnp.clip(entries, -bound, bound).astype(kind)


def setup_inputs(seed: int = 0) -> dict:
    seeds = jax.random.split(jax.random.key(seed), 8)
    return {
        "q_proj": draw_q_proj(jax.random.fold_in(seeds[7], 71), 0),
        "k_proj": draw_k_proj(jax.random.fold_in(seeds[7], 71), 0),
        "v_proj": scatter_about(seeds[2], (CLIPS, CT, HEADS * HD), 1.0, 6.0, ((0, 8), (1, 4))),
        "neighbours": draw_neighbours(jax.random.fold_in(seeds[7], 71), 0),
        "counts": draw_counts(jax.random.fold_in(seeds[7], 71), 0),
        "w_out": scatter_about(seeds[5], (HEADS * HD, D), (HEADS * HD) ** -0.5, 0.125, ((0, 32),)),
        "d_out": scatter_about(seeds[6], (CLIPS, CT, D), 1.0, 6.0, ((0, 8), (1, 4))),
    }


def attend_exact(qh, kh, vh, idx, valid, scale):
    nb = idx.shape[0]
    heads_here = qh.shape[1] // HD
    q_blocks = qh.reshape(nb, BLK, heads_here, HD).astype(jnp.float32)
    k_blocks = kh.reshape(nb, BLK, heads_here, HD)[idx].astype(jnp.float32)
    v_blocks = vh.reshape(nb, BLK, heads_here, HD)[idx].astype(jnp.float32)
    scores = jnp.einsum('bqhd,bskhd->bhqsk', q_blocks, k_blocks) * scale
    scores = jnp.where(valid[:, None, None, :, None], scores, -jnp.inf)
    top = lax.optimization_barrier(jnp.max(scores, axis=(3, 4), keepdims=True))
    expo = jnp.exp(scores - top)
    soft = expo / lax.optimization_barrier(jnp.sum(expo, axis=(3, 4), keepdims=True))
    probs = soft.astype(jnp.bfloat16)
    attn = jnp.einsum('bhqsk,bskhd->bqhd', probs.astype(jnp.float32), v_blocks).astype(jnp.bfloat16)
    return (attn.reshape(nb * BLK, heads_here * HD), (q_blocks, k_blocks, v_blocks, soft, probs))

def attend_back_exact(dattn, saved, idx, valid, scale):
    q_blocks, k_blocks, v_blocks, soft, probs = saved
    nb = idx.shape[0]
    heads_here = q_blocks.shape[2]
    d_blocks = dattn.reshape(nb, BLK, heads_here, HD).astype(jnp.float32)
    dprobs = jnp.einsum('bqhd,bskhd->bhqsk', d_blocks, v_blocks)
    dprobs = jnp.where(valid[:, None, None, :, None], dprobs, 0.0)
    delta = lax.optimization_barrier(jnp.sum(soft * dprobs, axis=(3, 4), keepdims=True))
    dsc = (soft * (dprobs - delta)).astype(jnp.bfloat16).astype(jnp.float32)
    grad_q = (jnp.einsum('bhqsk,bskhd->bqhd', dsc, k_blocks) * scale).astype(jnp.bfloat16)
    v_terms = jnp.einsum('bhqsk,bqhd->bskhd', probs.astype(jnp.float32), d_blocks)
    k_terms = jnp.einsum('bhqsk,bqhd->bskhd', dsc, q_blocks)
    owner = ((idx[:, :, None] == jnp.arange(nb)[None, None, :]) & valid[:, :, None]).astype(jnp.float32)
    grad_v = jnp.einsum('bsc,bskhd->ckhd', owner, v_terms, precision=lax.Precision.HIGHEST).astype(jnp.bfloat16)
    grad_k = (jnp.einsum('bsc,bskhd->ckhd', owner, k_terms, precision=lax.Precision.HIGHEST) * scale).astype(jnp.bfloat16)
    width = heads_here * HD
    return (grad_q.reshape(nb * BLK, width), grad_k.reshape(nb * BLK, width), grad_v.reshape(nb * BLK, width))

def reference(q_proj, k_proj, v_proj, neighbours, counts, w_out, d_out):
    scale = 1.0 / math.sqrt(HD)
    group = HEADS * HD // N_SEQ
    slot_ids = jnp.arange(MAXN)

    def step(accum, item):
        q_clip, k_clip, v_clip, nbr, cnt, d_clip = item
        valid = slot_ids[None, :] < cnt[:, None]
        attn, saved = attend_exact(q_clip, k_clip, v_clip, nbr, valid, scale)
        parts = [jnp.dot(attn[:, g * group:(g + 1) * group], w_out[g * group:(g + 1) * group], preferred_element_type=jnp.float32).astype(jnp.bfloat16) for g in range(N_SEQ)]
        parts = lax.optimization_barrier(parts)
        total = jnp.zeros((CT, D), jnp.float32)
        for part in parts:
            total = total + part.astype(jnp.float32)
        out_clip = total.astype(jnp.bfloat16)
        dattn = lax.dot_general(d_clip, w_out, (((1,), (1,)), ((), ())), preferred_element_type=jnp.float32).astype(jnp.bfloat16)
        term = lax.dot_general(attn, d_clip, (((0,), (0,)), ((), ())), preferred_element_type=jnp.float32).astype(jnp.bfloat16)
        term = lax.optimization_barrier(term)
        grad_q, grad_k, grad_v = attend_back_exact(dattn, saved, nbr, valid, scale)
        return (accum + term.astype(jnp.float32), (out_clip, grad_q, grad_k, grad_v))
    start = jnp.zeros((HEADS * HD, D), jnp.float32)
    grad_w, (out_y, grad_q, grad_k, grad_v) = lax.scan(step, start, (q_proj, k_proj, v_proj, neighbours, counts, d_out))
    return (out_y, grad_q, grad_k, grad_v, grad_w)
```

```python
import functools
import math

import jax
import jax.numpy as jnp
from jax import lax
from jax.experimental import pallas as pl
from jax.experimental.pallas import tpu as pltpu
from jax.sharding import PartitionSpec as P

HD = 128
BLK = 128
MB = 1 << 20
BF = jnp.bfloat16
F32 = jnp.float32


ANY = pl.BlockSpec(memory_space=pl.ANY)
SMEM = pl.BlockSpec(memory_space=pltpu.SMEM)


def params(mb):
    return pltpu.CompilerParams(vmem_limit_bytes=mb * MB)


def sds(shape, dtype=BF):
    return jax.ShapeDtypeStruct(shape, dtype)


def run_copies(copies):
    for c in copies:
        c.start()
    for c in copies:
        c.wait()


def pack_kernel(n, width, me_ref, q_ref, k_ref, v_ref, *rest):
    outs, sem = rest[: n - 1], rest[n - 1]
    me = me_ref[0]
    copies = []
    for r in range(1, n):
        col = pl.multiple_of((me ^ r) * width, 128)
        for t, src in enumerate((q_ref, k_ref, v_ref)):
            copies.append(
                pltpu.make_async_copy(
                    src.at[0, :, pl.ds(col, width)], outs[r - 1].at[t], sem.at[len(copies)]
                )
            )
    run_copies(copies)


def pack(me, q, k, v, n):
    rows, cols = q.shape[1:]
    width = cols // n
    return pl.pallas_call(
        functools.partial(pack_kernel, n, width),
        out_shape=[sds((3, rows, width))] * (n - 1),
        in_specs=[SMEM, ANY, ANY, ANY],
        out_specs=[ANY] * (n - 1),
        scratch_shapes=[pltpu.SemaphoreType.DMA((3 * (n - 1),))],
        name="pack",
    )(me, q, k, v)


def unpack_kernel(n, width, me_ref, *rest):
    parts, outs, sem = rest[:n], rest[n : n + 3], rest[n + 3]
    me = me_ref[0]
    copies = []
    for r in range(n):
        col = pl.multiple_of((me ^ r) * width, 128)
        for t in range(3):
            copies.append(
                pltpu.make_async_copy(
                    parts[r].at[t], outs[t].at[0, :, pl.ds(col, width)], sem.at[len(copies)]
                )
            )
    run_copies(copies)


def unpack(me, parts):
    n = len(parts)
    _, rows, width = parts[0].shape
    return pl.pallas_call(
        functools.partial(unpack_kernel, n, width),
        out_shape=[sds((1, rows, n * width))] * 3,
        in_specs=[SMEM] + [ANY] * n,
        out_specs=[ANY] * 3,
        scratch_shapes=[pltpu.SemaphoreType.DMA((3 * n,))],
        name="unpack",
    )(me, *parts)


def load_copies(me, rows, width, own, parts, held, sem):
    copies = []
    col = pl.multiple_of(me * width, 128)
    for t in range(3):
        copies.append(
            pltpu.make_async_copy(
                own[t].at[0, :, pl.ds(col, width)], held.at[t, pl.ds(0, rows)], sem.at[len(copies)]
            )
        )
    for r, part in enumerate(parts, 1):
        for t in range(3):
            copies.append(
                pltpu.make_async_copy(
                    part.at[t], held.at[t, pl.ds(r * rows, rows)], sem.at[len(copies)]
                )
            )
    return copies


def place(block, me, per):
    return pl.multiple_of((((block // per) ^ me) * per + block % per) * BLK, BLK)


def soft_of(q, ks, used, scale):
    scores = []
    for j, kj in enumerate(ks):
        s = lax.dot_general(q, kj, (((1,), (1,)), ((), ())), preferred_element_type=F32) * scale
        scores.append(s if j == 0 else jnp.where(used[j], s, -jnp.inf))
    top = functools.reduce(jnp.maximum, scores)
    top = jnp.max(top, axis=1, keepdims=True)
    expo = [jnp.exp(s - top) for s in scores]
    total = jnp.sum(functools.reduce(jnp.add, expo), axis=1, keepdims=True)
    inv = 1.0 / total
    return [e * inv for e in expo]


def fwd_kernel(n, per, heads, slots, scale, me_ref, nbr_ref, cnt_ref, q_ref, k_ref, v_ref, *rest):
    parts = rest[: n - 1]
    attn_ref, swap_ref, held, sem = rest[n - 1 :]
    me = me_ref[0]
    rows, width = per * BLK, heads * HD
    run_copies(load_copies(me, rows, width, (q_ref, k_ref, v_ref), parts, held, sem))

    def block(b, _):
        at = place(b, me, per)
        cnt = cnt_ref[0, b]
        used = [j < cnt for j in range(slots)]
        keys = [place(nbr_ref[0, b, j], me, per) for j in range(slots)]
        there = pl.multiple_of(place(b, me ^ 1, per), BLK)
        for h in range(heads):
            c = slice(h * HD, (h + 1) * HD)
            q = held[0, pl.ds(at, BLK), c]
            ks = [held[1, pl.ds(e, BLK), c] for e in keys]
            vs = [held[2, pl.ds(e, BLK), c] for e in keys]
            soft = soft_of(q, ks, used, scale)
            out = functools.reduce(
                jnp.add,
                [jnp.dot(s.astype(BF), vj, preferred_element_type=F32) for s, vj in zip(soft, vs)],
            ).astype(BF)
            attn_ref[pl.ds(at, BLK), c] = out
            swap_ref[pl.ds(there, BLK), c] = out
        return 0

    lax.fori_loop(0, n * per, block, 0)


def attend(me, nbr, cnt, q, k, v, parts, scale):
    n = len(parts) + 1
    _, rows, width = parts[0].shape
    per, heads, slots = rows // BLK, width // HD, nbr.shape[2]
    vm = pl.BlockSpec(memory_space=pltpu.VMEM)
    return pl.pallas_call(
        functools.partial(fwd_kernel, n, per, heads, slots, scale),
        out_shape=[sds((n * rows, width))] * 2,
        in_specs=[SMEM] * 3 + [ANY] * (n + 2),
        out_specs=[vm, vm],
        scratch_shapes=[pltpu.VMEM((3, n * rows, width), BF), pltpu.SemaphoreType.DMA((3 * n,))],
        compiler_params=params(32),
        cost_estimate=pl.CostEstimate(flops=14 * 10**9, bytes_accessed=8 * MB, transcendentals=0),
        name="attend",
    )(me, nbr, cnt, q, k, v, *parts)


def bwd_kernel(
    n, per, heads, slots, scale, me_ref, nbr_ref, cnt_ref, q_ref, k_ref, v_ref, *rest
):
    parts = rest[: n - 1]
    mine_ref, other_ref = rest[n - 1 : n + 1]
    outs = rest[n + 1 : 2 * n + 1]
    held, dk, dv, sem = rest[2 * n + 1 :]
    me = me_ref[0]
    rows, width = per * BLK, heads * HD
    copies = load_copies(me, rows, width, (q_ref, k_ref, v_ref), parts, held, sem)
    for c in copies:
        c.start()
    dk[...] = jnp.zeros_like(dk)
    dv[...] = jnp.zeros_like(dv)
    for c in copies:
        c.wait()

    def block(b, _):
        at = place(b, me, per)
        cnt = cnt_ref[0, b]
        used = [j < cnt for j in range(slots)]
        keys = [place(nbr_ref[0, b, j], me, per) for j in range(slots)]
        for h in range(heads):
            c = slice(h * HD, (h + 1) * HD)
            q = held[0, pl.ds(at, BLK), c]
            ks = [held[1, pl.ds(e, BLK), c] for e in keys]
            vs = [held[2, pl.ds(e, BLK), c] for e in keys]
            soft = soft_of(q, ks, used, scale)
            d = (
                mine_ref[pl.ds(at, BLK), c].astype(F32) + other_ref[pl.ds(at, BLK), c].astype(F32)
            ).astype(BF)
            dp = [
                lax.dot_general(d, vj, (((1,), (1,)), ((), ())), preferred_element_type=F32)
                for vj in vs
            ]
            delta = jnp.sum(
                functools.reduce(jnp.add, [s * p for s, p in zip(soft, dp)]), axis=1, keepdims=True
            )
            ds = [(s * (p - delta)).astype(BF) for s, p in zip(soft, dp)]
            dq = functools.reduce(
                jnp.add, [jnp.dot(x, kj, preferred_element_type=F32) for x, kj in zip(ds, ks)]
            )
            held[0, pl.ds(at, BLK), c] = (dq * scale).astype(BF)
            for e, s, x in zip(keys, soft, ds):
                over = (((0,), (0,)), ((), ()))
                dv[pl.ds(e, BLK), c] += lax.dot_general(
                    s.astype(BF), d, over, preferred_element_type=F32
                )
                dk[pl.ds(e, BLK), c] += lax.dot_general(x, q, over, preferred_element_type=F32)
        return 0

    lax.fori_loop(0, n * per, block, 0)
    for r in range(n):
        here = slice(r * rows, (r + 1) * rows)
        outs[r][0] = held[0, here]
        outs[r][1] = (dk[here] * scale).astype(BF)
        outs[r][2] = dv[here].astype(BF)


def attend_back(me, nbr, cnt, q, k, v, parts, mine, other, scale):
    n = len(parts) + 1
    _, rows, width = parts[0].shape
    per, heads, slots = rows // BLK, width // HD, nbr.shape[2]
    vm = pl.BlockSpec(memory_space=pltpu.VMEM)
    return pl.pallas_call(
        functools.partial(bwd_kernel, n, per, heads, slots, scale),
        out_shape=[sds((3, rows, width))] * n,
        in_specs=[SMEM] * 3 + [ANY] * (n + 2) + [vm, vm],
        out_specs=[vm] * n,
        scratch_shapes=[
            pltpu.VMEM((3, n * rows, width), BF),
            pltpu.VMEM((n * rows, width), F32),
            pltpu.VMEM((n * rows, width), F32),
            pltpu.SemaphoreType.DMA((3 * n,)),
        ],
        compiler_params=params(40),
        cost_estimate=pl.CostEstimate(flops=28 * 10**9, bytes_accessed=12 * MB, transcendentals=0),
        name="attend_back",
    )(me, nbr, cnt, q, k, v, *parts, mine, other)


def project_kernel(a_ref, b_ref, wa_ref, wb_ref, o_ref):
    o_ref[...] = (
        jnp.dot(a_ref[...], wa_ref[...], preferred_element_type=F32)
        + jnp.dot(b_ref[...], wb_ref[...], preferred_element_type=F32)
    ).astype(o_ref.dtype)


def project(a, b, wa, wb, half, tile=512):
    rows, depth = a.shape
    rows //= 2
    cols = wa.shape[1]
    left = pl.BlockSpec((rows, depth), lambda j: (half, 0))
    right = pl.BlockSpec((depth, tile), lambda j: (0, j))
    return pl.pallas_call(
        project_kernel,
        grid=(cols // tile,),
        out_shape=sds((rows, cols)),
        in_specs=[left, left, right, right],
        out_specs=pl.BlockSpec((rows, tile), lambda j: (0, j)),
        compiler_params=params(32),
        cost_estimate=pl.CostEstimate(
            flops=4 * rows * depth * cols, bytes_accessed=10 * MB, transcendentals=0
        ),
        name="project",
    )(a, b, wa, wb)


def project_back_kernel(n, order, *refs):
    ds, w_ref, o_ref = refs[:n], refs[n], refs[n + 1]
    i = pl.program_id(0)
    for r in range(n):

        @pl.when(i == r)
        def _(d_ref=ds[order[r]]):
            o_ref[...] = lax.dot_general(
                d_ref[...], w_ref[...], (((1,), (1,)), ((), ())), preferred_element_type=F32
            ).astype(o_ref.dtype)


def project_back(ds, w, order):
    n = len(ds)
    rows, cols = ds[0].shape
    width = w.shape[0]
    return pl.pallas_call(
        functools.partial(project_back_kernel, n, order),
        grid=(n,),
        out_shape=sds((n * rows, width)),
        in_specs=[pl.BlockSpec((rows, cols), lambda i: (0, 0))] * n
        + [pl.BlockSpec((width, cols), lambda i: (0, 0))],
        out_specs=pl.BlockSpec((rows, width), lambda i: (i, 0)),
        compiler_params=params(40),
        cost_estimate=pl.CostEstimate(
            flops=2 * n * rows * width * cols, bytes_accessed=10 * MB, transcendentals=0
        ),
        name="project_back",
    )(*ds, w)


def weight_kernel(n, a_ref, b_ref, *refs):
    ds, oa_ref, ob_ref, at, bt = refs[:n], refs[n], refs[n + 1], refs[n + 2], refs[n + 3]
    rows = ds[0].shape[0]

    @pl.when(pl.program_id(0) == 0)
    def _():
        at[...] = a_ref[...].T
        bt[...] = b_ref[...].T

    for t, o_ref in ((at, oa_ref), (bt, ob_ref)):
        o_ref[...] = functools.reduce(
            jnp.add,
            [
                jnp.dot(t[:, r * rows : (r + 1) * rows], d[...], preferred_element_type=F32)
                for r, d in enumerate(ds)
            ],
        ).astype(o_ref.dtype)


def weight_grad(a, b, ds, tile=512):
    n = len(ds)
    tokens, width = a.shape
    rows, cols = ds[0].shape
    whole = pl.BlockSpec((tokens, width), lambda j: (0, 0))
    out = pl.BlockSpec((width, tile), lambda j: (0, j))
    return pl.pallas_call(
        functools.partial(weight_kernel, n),
        grid=(cols // tile,),
        out_shape=[sds((width, cols))] * 2,
        in_specs=[whole, whole] + [pl.BlockSpec((rows, tile), lambda j: (0, j))] * n,
        out_specs=[out, out],
        scratch_shapes=[pltpu.VMEM((width, tokens), BF)] * 2,
        compiler_params=params(40),
        cost_estimate=pl.CostEstimate(
            flops=4 * tokens * width * cols, bytes_accessed=14 * MB, transcendentals=0
        ),
        name="weight_grad",
    )(a, b, *ds)


def on_device(n, q_proj, k_proj, v_proj, neighbours, counts, w_out, d_out):
    scale = 1.0 / math.sqrt(HD)
    seq = lax.axis_index("seq")
    me = seq.astype(jnp.int32)[None]
    half = d_out.shape[2] // 2
    low = seq & 1

    def to(x, r):
        return lax.ppermute(x, "seq", [(i, i ^ r) for i in range(n)])

    def mine(x):
        return lax.dynamic_slice_in_dim(x, low * half, half, 1)

    def theirs(x):
        return lax.dynamic_slice_in_dim(x, (1 - low) * half, half, 1)

    w_pair = to(theirs(w_out), 1)
    w_a = lax.all_gather(mine(w_out), "zero", axis=0, tiled=True)
    w_b = lax.all_gather(w_pair, "zero", axis=0, tiled=True)

    sent = pack(me, q_proj, k_proj, v_proj, n)
    parts = [to(x, r) for r, x in enumerate(sent, 1)]

    d_local = d_out[0]
    d0 = mine(d_local)
    d1 = to(theirs(d_local), 1)
    d2 = to(d0, 2)
    d3 = to(d1, 2)
    ds = [d0, d1, d2, d3]

    attn, swapped = attend(me, neighbours, counts, q_proj, k_proj, v_proj, parts, scale)
    attn_pair = to(swapped, 1)

    back_pair = to(project_back(ds, w_b, (1, 0, 3, 2)), 1)
    back_own = project_back(ds, w_a, (0, 1, 2, 3))

    y_far = to(project(attn, attn_pair, w_a, w_b, 1), 2)
    y_near = project(attn, attn_pair, w_a, w_b, 0)
    y = (y_near.astype(F32) + y_far.astype(F32)).astype(BF)
    rows = y.shape[0] // 2
    y_pair = to(y[rows:], 1)
    y_own = y[:rows]
    out_y = jnp.where(
        low == 0,
        jnp.concatenate([y_own, y_pair], axis=1),
        jnp.concatenate([y_pair, y_own], axis=1),
    )[None]

    gw_a, gw_b = weight_grad(attn, attn_pair, ds)
    gw_a = lax.psum_scatter(gw_a, "zero", scatter_dimension=0, tiled=True)
    gw_b = lax.psum_scatter(gw_b, "zero", scatter_dimension=0, tiled=True)
    gw_pair = to(gw_b, 1)
    grad_w = jnp.where(
        low == 0,
        jnp.concatenate([gw_a, gw_pair], axis=1),
        jnp.concatenate([gw_pair, gw_a], axis=1),
    ).astype(F32)

    grads = attend_back(
        me, neighbours, counts, q_proj, k_proj, v_proj, parts, back_own, back_pair, scale
    )
    grads = [grads[0]] + [to(x, r) for r, x in enumerate(grads[1:], 1)]
    grad_q, grad_k, grad_v = unpack(me, grads)
    return (out_y, grad_q, grad_k, grad_v, grad_w)


def solution(mesh):
    return jax.shard_map(
        functools.partial(on_device, mesh.shape["seq"]),
        mesh=mesh,
        in_specs=(
            P("zero", "seq", None),
            P("zero", "seq", None),
            P("zero", "seq", None),
            P("zero", None, None),
            P("zero", None),
            P(("seq", "zero"), None),
            P("zero", "seq", None),
        ),
        out_specs=(
            P("zero", "seq", None),
            P("zero", "seq", None),
            P("zero", "seq", None),
            P("zero", "seq", None),
            P(("seq", "zero"), None),
        ),
        check_vma=False,
    )
```

```python
import functools
import math

import jax
import jax.numpy as jnp
from jax import lax
from jax.experimental import pallas as pl
from jax.experimental.pallas import tpu as pltpu
from jax.sharding import PartitionSpec as P

HD = 128
BLK = 128
MB = 1 << 20
BF = jnp.bfloat16
COST = pl.CostEstimate(flops=1024, bytes_accessed=1024, transcendentals=0)
LONG = pl.CostEstimate(flops=1024, bytes_accessed=1024, transcendentals=0)
F32 = jnp.float32


ANY = pl.BlockSpec(memory_space=pl.ANY)
SMEM = pl.BlockSpec(memory_space=pltpu.SMEM)


def params(mb):
    return pltpu.CompilerParams(vmem_limit_bytes=mb * MB)


def sds(shape, dtype=BF):
    return jax.ShapeDtypeStruct(shape, dtype)


def run_copies(copies):
    for c in copies:
        c.start()
    for c in copies:
        c.wait()


def staged(moves, *rest):
    held, sem_in, sem_out = rest[:-2], rest[-2], rest[-1]
    ins = [pltpu.make_async_copy(a, h, sem_in.at[i]) for i, ((a, _), h) in enumerate(zip(moves, held))]
    outs = [pltpu.make_async_copy(h, b, sem_out.at[i]) for i, ((_, b), h) in enumerate(zip(moves, held))]
    for c in ins:
        c.start()
    for c, o in zip(ins, outs):
        c.wait()
        o.start()
    for o in outs:
        o.wait()


def pack_kernel(q_ref, k_ref, v_ref, out_ref, *rest):
    n, _, _, width = out_ref.shape
    moves = [
        (src.at[0, :, pl.ds(g * width, width)], out_ref.at[g, t])
        for g in range(n)
        for t, src in enumerate((q_ref, k_ref, v_ref))
    ]
    staged(moves, *rest)


def pack(q, k, v, n):
    rows, cols = q.shape[1:]
    width = cols // n
    return pl.pallas_call(
        pack_kernel,
        out_shape=sds((n, 3, rows, width)),
        in_specs=[ANY, ANY, ANY],
        out_specs=ANY,
        scratch_shapes=[pltpu.VMEM((rows, width), BF)] * (3 * n)
        + [pltpu.SemaphoreType.DMA((3 * n,))] * 2,
        compiler_params=params(60),
        cost_estimate=COST,
        name="pack",
    )(q, k, v)


def unpack_kernel(n, width, cuts, me_ref, *rest):
    m = n * len(cuts)
    parts, outs = rest[:m], rest[m : m + 3]
    moves = []
    for i, part in enumerate(parts):
        col = pl.multiple_of((me_ref[0] ^ (i % n)) * width + cuts[i // n], 128)
        for t in range(3):
            moves.append((part.at[t], outs[t].at[0, :, pl.ds(col, part.shape[2])]))
    staged(moves, *rest[m + 3 :])


def unpack(me, chunks):
    n = len(chunks[0])
    cuts = [sum(c[0].shape[2] for c in chunks[:i]) for i in range(len(chunks))]
    width = sum(c[0].shape[2] for c in chunks)
    rows = chunks[0][0].shape[1]
    parts = [x for c in chunks for x in c]
    return pl.pallas_call(
        functools.partial(unpack_kernel, n, width, cuts),
        out_shape=[sds((1, rows, n * width))] * 3,
        in_specs=[SMEM] + [ANY] * len(parts),
        out_specs=[ANY] * 3,
        scratch_shapes=[pltpu.VMEM(x.shape[1:], BF) for x in parts for _ in range(3)]
        + [pltpu.SemaphoreType.DMA((3 * len(parts),))] * 2,
        compiler_params=params(60),
        cost_estimate=LONG,
        name="unpack",
    )(me, *parts)


def join_kernel(width, low_ref, *rest):
    m = (len(rest) - 3) // 2
    parts, out = rest[:m], rest[m]
    moves, col = [], 0
    for i, part in enumerate(parts):
        if i == m // 2:
            col = 0
        side = low_ref[0] if i < m // 2 else 1 - low_ref[0]
        start = pl.multiple_of(side * width + col, 128)
        col += part.shape[1]
        moves.append((part, out.at[0, :, pl.ds(start, part.shape[1])]))
    staged(moves, *rest[m + 1 :])


def join(low, own, pair):
    parts = own + pair
    rows = parts[0].shape[0]
    width = sum(x.shape[1] for x in own)
    return pl.pallas_call(
        functools.partial(join_kernel, width),
        out_shape=sds((1, rows, 2 * width)),
        in_specs=[SMEM] + [ANY] * len(parts),
        out_specs=ANY,
        scratch_shapes=[pltpu.VMEM(x.shape, BF) for x in parts]
        + [pltpu.SemaphoreType.DMA((len(parts),))] * 2,
        compiler_params=params(60),
        cost_estimate=LONG,
        name="join",
    )(low, *parts)


def place(block, me, per):
    return pl.multiple_of((((block // per) ^ me) * per + block % per) * BLK, BLK)


NT = (((1,), (1,)), ((), ()))
TN = (((0,), (0,)), ((), ()))


def dot(a, b, dims=(((1,), (0,)), ((), ()))):
    return lax.dot_general(a, b, dims, preferred_element_type=F32)


def soft_of(scores, axis):
    expo = jnp.exp(scores - jnp.max(scores, axis=axis, keepdims=True))
    return expo * (1.0 / jnp.sum(expo, axis=axis, keepdims=True))


def for_blocks(blocks, slots, nbr_ref, cnt_ref, body):
    def block(b, _):
        for count in range(1, slots + 1):

            @pl.when(cnt_ref[0, b] == count)
            def _():
                body(b, [nbr_ref[0, b, j] for j in range(count)])

        return 0

    lax.fori_loop(0, blocks, block, 0)


def gather(held, t, keys, per, out):
    for j, e in enumerate(keys):
        rows = pl.ds(pl.multiple_of(e % per * BLK, BLK), BLK)
        out[j * BLK : (j + 1) * BLK] = held[e // per, t, rows]


def fwd_kernel(heads, slots, scale, me_ref, nbr_ref, cnt_ref, held, attn_ref, swap_ref, ks, vs):
    me = me_ref[0]
    n, per = held.shape[0], held.shape[2] // BLK

    def body(b, keys):
        here, there = place(b, me, per), place(b, me ^ 1, per)
        rows = pl.ds(pl.multiple_of(b % per * BLK, BLK), BLK)
        gather(held, 1, keys, per, ks)
        gather(held, 2, keys, per, vs)
        used = slice(0, len(keys) * BLK)
        cols = [slice(h * HD, (h + 1) * HD) for h in range(heads)]
        scores = [dot(held[b // per, 0, rows, c], ks[used, c], NT) * scale for c in cols]
        probs = [soft_of(x, 1).astype(BF) for x in scores]
        for c, p in zip(cols, probs):
            out = dot(p, vs[used, c]).astype(BF)
            attn_ref[pl.ds(here, BLK), c] = out
            swap_ref[pl.ds(there, BLK), c] = out

    for_blocks(n * per, slots, nbr_ref, cnt_ref, body)


def attend(me, nbr, cnt, got, scale):
    n, _, rows, width = got.shape
    vm = pl.BlockSpec(memory_space=pltpu.VMEM)
    return pl.pallas_call(
        functools.partial(fwd_kernel, width // HD, nbr.shape[2], scale),
        out_shape=[sds((n * rows, width))] * 2,
        in_specs=[SMEM] * 3 + [vm],
        out_specs=[vm, vm],
        scratch_shapes=[pltpu.VMEM((nbr.shape[2] * BLK, width), BF)] * 2,
        compiler_params=params(60),
        cost_estimate=COST,
        name="attend",
    )(me, nbr, cnt, got)


def bwd_kernel(begin, slots, scale, me_ref, nbr_ref, cnt_ref, got_ref, *rest):
    d_refs, outs, (held, terms, dq, dk, dv, ks, vs, sem, d_sem) = rest[:4], rest[4:-9], rest[-9:]
    me = me_ref[0]
    n, _, rows, some = held.shape
    per = rows // BLK
    cols = pl.ds(begin, some)
    copies = [pltpu.make_async_copy(got_ref.at[:, :, :, cols], held, sem)]
    for i, ref in enumerate(d_refs):
        part = pl.ds(i % 2 * ref.shape[0], ref.shape[0])
        copies.append(
            pltpu.make_async_copy(ref.at[:, cols], terms.at[i // 2, part], d_sem.at[i])
        )
    for c in copies:
        c.start()
    dk[...] = jnp.zeros_like(dk)
    dv[...] = jnp.zeros_like(dv)
    for c in copies:
        c.wait()

    def body(b, keys):
        here = pl.ds(place(b, me, per), BLK)
        rows_b = pl.ds(pl.multiple_of(b % per * BLK, BLK), BLK)
        gather(held, 1, keys, per, ks)
        gather(held, 2, keys, per, vs)
        used = slice(0, len(keys) * BLK)
        heads = [slice(h * HD, (h + 1) * HD) for h in range(some // HD)]
        qs = [held[b // per, 0, rows_b, c] for c in heads]
        ds = [
            (terms[0, here, c].astype(F32) + terms[1, here, c].astype(F32)).astype(BF)
            for c in heads
        ]
        softs = [soft_of(dot(ks[used, c], q, NT) * scale, 0) for c, q in zip(heads, qs)]
        dps = [dot(vs[used, c], d, NT) for c, d in zip(heads, ds)]
        dss = [
            (s * (p - jnp.sum(s * p, axis=0, keepdims=True))).astype(BF)
            for s, p in zip(softs, dps)
        ]
        for c, q, d, s, x in zip(heads, qs, ds, softs, dss):
            dq[b // per, rows_b, c] = (dot(x, ks[used, c], TN) * scale).astype(BF)
            to_v, to_k = dot(s.astype(BF), d), dot(x, q)
            for j, e in enumerate(keys):
                rows_e = pl.ds(pl.multiple_of(e * BLK, BLK), BLK)
                dv[rows_e, c] += to_v[j * BLK : (j + 1) * BLK]
                dk[rows_e, c] += to_k[j * BLK : (j + 1) * BLK]

    for_blocks(n * per, slots, nbr_ref, cnt_ref, body)
    for r, out in enumerate(outs):
        g = me ^ r
        rows_g = pl.ds(pl.multiple_of(g * rows, BLK), rows)
        out[0] = dq[g]
        out[1] = (dk[rows_g] * scale).astype(BF)
        out[2] = dv[rows_g].astype(BF)


def attend_back(me, nbr, cnt, got, terms, begin, end, scale):
    n, _, rows, _ = got.shape
    some = end - begin
    vm = pl.BlockSpec(memory_space=pltpu.VMEM)
    return pl.pallas_call(
        functools.partial(bwd_kernel, begin, nbr.shape[2], scale),
        out_shape=[sds((3, rows, some))] * n,
        in_specs=[SMEM] * 3 + [ANY] * 5,
        out_specs=[vm] * n,
        scratch_shapes=[
            pltpu.VMEM((n, 3, rows, some), BF),
            pltpu.VMEM((2, n * rows, some), BF),
            pltpu.VMEM((n, rows, some), BF),
            pltpu.VMEM((n * rows, some), F32),
            pltpu.VMEM((n * rows, some), F32),
            pltpu.VMEM((nbr.shape[2] * BLK, some), BF),
            pltpu.VMEM((nbr.shape[2] * BLK, some), BF),
            pltpu.SemaphoreType.DMA,
            pltpu.SemaphoreType.DMA((4,)),
        ],
        compiler_params=params(60),
        cost_estimate=COST,
        name="attend_back",
    )(me, nbr, cnt, got, *terms)


def project_kernel(a_ref, b_ref, wa_ref, wb_ref, *rest):
    y = dot(a_ref[...], wa_ref[...]) + dot(b_ref[...], wb_ref[...])
    if len(rest) == 1:
        rest[0][...] = y.astype(BF)
        return
    far_ref, own_ref, pair_ref = rest
    y = (y + far_ref[...].astype(F32)).astype(BF)
    rows = own_ref.shape[0]
    own_ref[...] = y[:rows]
    pair_ref[...] = y[rows:]


def project(a, b, wa, wb, part, parts, far=None, tile=640):
    rows, depth = a.shape
    rows //= 2
    cols = wa.shape[1] // parts
    skip = part * (cols // tile)
    near = far is not None
    left = pl.BlockSpec((rows, depth), lambda j: (0 if near else 1, 0))
    right = pl.BlockSpec((depth, tile), lambda j: (0, skip + j))
    out = rows // 2 if near else rows
    return pl.pallas_call(
        project_kernel,
        grid=(cols // tile,),
        out_shape=[sds((out, cols))] * (2 if near else 1),
        in_specs=[left, left, right, right]
        + [pl.BlockSpec((rows, tile), lambda j: (0, j))] * int(near),
        out_specs=[pl.BlockSpec((out, tile), lambda j: (0, j))] * (2 if near else 1),
        compiler_params=params(60),
        cost_estimate=LONG if near else COST,
        name="project",
    )(a, b, wa, wb, *([far] if near else []))


def project_back_kernel(n, m, order, *refs):
    d_refs, w_refs, o_refs = refs[:n], refs[n : n + m], refs[n + m : n + 2 * m]
    held_d, held_w, sem = refs[n + 2 * m :]
    rows = d_refs[0].shape[0]
    copies = [
        pltpu.make_async_copy(d, held_d.at[pl.ds(i * rows, rows)], sem.at[i])
        for i, d in enumerate(d_refs)
    ] + [pltpu.make_async_copy(w, held_w.at[i], sem.at[n + i]) for i, w in enumerate(w_refs)]
    for c in copies:
        c.start()
    for c in copies[: n + 1]:
        c.wait()
    for i in range(m):
        if i:
            copies[n + i].wait()
        out = dot(held_d[...], held_w[i], NT).astype(BF)
        for r in range(n):
            there = r ^ 1 if order[i] else r
            o_refs[i][there * rows : (there + 1) * rows] = out[r * rows : (r + 1) * rows]


def project_back(ds, ws, order):
    n, m = len(ds), len(ws)
    rows, cols = ds[0].shape
    width = ws[0].shape[0]
    vm = pl.BlockSpec(memory_space=pltpu.VMEM)
    return pl.pallas_call(
        functools.partial(project_back_kernel, n, m, order),
        out_shape=[sds((n * rows, width))] * m,
        in_specs=[ANY] * (n + m),
        out_specs=[vm] * m,
        scratch_shapes=[
            pltpu.VMEM((n * rows, cols), BF),
            pltpu.VMEM((m, width, cols), BF),
            pltpu.SemaphoreType.DMA((n + m,)),
        ],
        compiler_params=params(60),
        cost_estimate=COST,
        name="project_back",
    )(*ds, *ws)


def weight_kernel(n, a_ref, b_ref, *refs):
    ds, o_ref, at, bt, d = refs[:n], refs[n], refs[n + 1], refs[n + 2], refs[n + 3]
    rows = ds[0].shape[0]

    @pl.when(pl.program_id(0) == 0)
    def _():
        at[...] = a_ref[...].T
        bt[...] = b_ref[...].T

    for r, piece in enumerate(ds):
        d[r * rows : (r + 1) * rows] = piece[...]
    for i, t in enumerate((at, bt)):
        out = dot(t[...], d[...]).astype(BF)
        o_ref[:, i] = out.reshape(o_ref.shape[0], *o_ref.shape[2:])


def weight_grad(a, b, ds, owners, tile=512):
    n = len(ds)
    tokens, width = a.shape
    rows, cols = ds[0].shape
    some = width // owners
    apart = owners if some % 16 == 0 else 1
    whole = pl.BlockSpec((tokens, width), lambda j: (0, 0))
    out = pl.pallas_call(
        functools.partial(weight_kernel, n),
        grid=(cols // tile,),
        out_shape=sds((apart, 2, width // apart, cols)),
        in_specs=[whole, whole] + [pl.BlockSpec((rows, tile), lambda j: (0, j))] * n,
        out_specs=pl.BlockSpec((apart, 2, width // apart, tile), lambda j: (0, 0, 0, j)),
        scratch_shapes=[pltpu.VMEM((width, tokens), BF)] * 2 + [pltpu.VMEM((tokens, tile), BF)],
        compiler_params=params(60),
        cost_estimate=COST,
        name="weight_grad",
    )(a, b, *ds)
    if apart == 1:
        out = out.reshape(2, owners, some, cols).swapaxes(0, 1)
    return out.reshape(2 * width, cols)


def on_device(n, owners, q_proj, k_proj, v_proj, neighbours, counts, w_out, d_out):
    scale = 1.0 / math.sqrt(HD)
    seq = lax.axis_index("seq")
    me = seq.astype(jnp.int32)[None]
    half = d_out.shape[2] // 2
    low = seq & 1

    def to(x, r):
        return lax.ppermute(x, "seq", [(i, i ^ r) for i in range(n)])

    def mine(x):
        return lax.dynamic_slice_in_dim(x, low * half, half, 1)

    def theirs(x):
        return lax.dynamic_slice_in_dim(x, (1 - low) * half, half, 1)

    def after(x, *others):
        return lax.optimization_barrier((x, *others))[0]

    def exchange(x):
        return lax.all_to_all(x, "seq", split_axis=0, concat_axis=0, tiled=True)

    sent = pack(q_proj, k_proj, v_proj, n)
    got = exchange(sent)

    w_a = lax.all_gather(mine(w_out), "zero", axis=0, tiled=True)
    w_pair = after(to(theirs(after(w_out, sent)), 1), w_a, got)
    w_b = lax.all_gather(w_pair, "zero", axis=0, tiled=True)

    d_local = after(d_out, sent)[0]
    d0 = mine(d_local)
    d1 = to(theirs(d_local), 1)
    d2 = to(d0, 2)

    attn, swapped = attend(me, neighbours, counts, got, scale)
    attn_pair = to(swapped, 1)
    d3 = to(after(d1, attn), 2)

    sent_0, own_0 = project_back([d0, d1], [w_b, w_a], (1, 0))
    (sent_1,) = project_back([after(d2, sent_0), d3], [w_b], (1,))
    pair_0, pair_1 = to(sent_0, 1), to(sent_1, 1)

    attn_pair = after(attn_pair, sent_1)
    pieces = 2
    y_far = [project(attn, attn_pair, w_a, w_b, i, pieces)[0] for i in range(pieces)]
    after_far = after(attn_pair, *y_far)
    y_far = [to(y, 2) for y in y_far]

    (own_1,) = project_back([after(d2, after_far), d3], [w_a], (0,))

    gw = weight_grad(attn, after(after_far, own_1), [d0, d1, d2, d3], owners)

    terms = [own_0, after(own_1, gw), pair_0, pair_1]
    grads = attend_back(me, neighbours, counts, got, terms, 0, attn.shape[1], scale)
    back = [grads[0]] + [to(x, r) for r, x in enumerate(grads[1:], 1)]

    attn = after(attn, grads[0])
    ys = [project(attn, attn_pair, w_a, w_b, i, pieces, far) for i, far in enumerate(y_far)]
    y_own, y_pair = [y[0] for y in ys], [to(y[1], 1) for y in ys]
    out_y = join(low.astype(jnp.int32)[None], y_own, y_pair)
    grad_q, grad_k, grad_v = unpack(me, [back])

    gw = lax.psum_scatter(after(gw, y_far[0], pair_0, pair_1), "zero", scatter_dimension=0, tiled=True)
    gw = after(gw, grads[0])
    rows = gw.shape[0] // 2
    gw_own, gw_pair = gw[:rows], to(gw[rows:], 1)
    grad_w = jnp.where(
        low == 0,
        jnp.concatenate([gw_own, gw_pair], axis=1),
        jnp.concatenate([gw_pair, gw_own], axis=1),
    ).astype(F32)
    return (out_y, grad_q, grad_k, grad_v, grad_w)


def solution(mesh):
    return jax.shard_map(
        functools.partial(on_device, mesh.shape["seq"], mesh.shape["zero"]),
        mesh=mesh,
        in_specs=(
            P("zero", "seq", None),
            P("zero", "seq", None),
            P("zero", "seq", None),
            P("zero", None, None),
            P("zero", None),
            P(("seq", "zero"), None),
            P("zero", "seq", None),
        ),
        out_specs=(
            P("zero", "seq", None),
            P("zero", "seq", None),
            P("zero", "seq", None),
            P("zero", "seq", None),
            P(("seq", "zero"), None),
        ),
        check_vma=False,
    )
```

```python
import functools
import math

import jax
import jax.numpy as jnp
from jax import lax
from jax.experimental import pallas as pl
from jax.experimental.pallas import tpu as pltpu
from jax.sharding import PartitionSpec as P

HD = 128
BLK = 128
MB = 1 << 20
BF = jnp.bfloat16
COST = pl.CostEstimate(flops=1024, bytes_accessed=1024, transcendentals=0)
LONG = pl.CostEstimate(flops=1024, bytes_accessed=1024, transcendentals=0)
F32 = jnp.float32


ANY = pl.BlockSpec(memory_space=pl.ANY)
SMEM = pl.BlockSpec(memory_space=pltpu.SMEM)


def params(mb):
    return pltpu.CompilerParams(vmem_limit_bytes=mb * MB)


def sds(shape, dtype=BF):
    return jax.ShapeDtypeStruct(shape, dtype)


def run_copies(copies):
    for c in copies:
        c.start()
    for c in copies:
        c.wait()


def staged(moves, *rest):
    held, sem_in, sem_out = rest[:-2], rest[-2], rest[-1]
    ins = [pltpu.make_async_copy(a, h, sem_in.at[i]) for i, ((a, _), h) in enumerate(zip(moves, held))]
    outs = [pltpu.make_async_copy(h, b, sem_out.at[i]) for i, ((_, b), h) in enumerate(zip(moves, held))]
    for c in ins:
        c.start()
    for c, o in zip(ins, outs):
        c.wait()
        o.start()
    for o in outs:
        o.wait()


def pack_kernel(q_ref, k_ref, v_ref, out_ref, *rest):
    n, _, _, width = out_ref.shape
    moves = [
        (src.at[0, :, pl.ds(g * width, width)], out_ref.at[g, t])
        for g in range(n)
        for t, src in enumerate((q_ref, k_ref, v_ref))
    ]
    staged(moves, *rest)


def pack(q, k, v, n):
    rows, cols = q.shape[1:]
    width = cols // n
    return pl.pallas_call(
        pack_kernel,
        out_shape=sds((n, 3, rows, width)),
        in_specs=[ANY, ANY, ANY],
        out_specs=ANY,
        scratch_shapes=[pltpu.VMEM((rows, width), BF)] * (3 * n)
        + [pltpu.SemaphoreType.DMA((3 * n,))] * 2,
        compiler_params=params(60),
        cost_estimate=COST,
        name="pack",
    )(q, k, v)


def unpack_kernel(n, width, cuts, me_ref, *rest):
    m = n * len(cuts)
    parts, outs = rest[:m], rest[m : m + 3]
    moves = []
    for i, part in enumerate(parts):
        col = pl.multiple_of((me_ref[0] ^ (i % n)) * width + cuts[i // n], 128)
        for t in range(3):
            moves.append((part.at[t], outs[t].at[0, :, pl.ds(col, part.shape[2])]))
    staged(moves, *rest[m + 3 :])


def unpack(me, chunks):
    n = len(chunks[0])
    cuts = [sum(c[0].shape[2] for c in chunks[:i]) for i in range(len(chunks))]
    width = sum(c[0].shape[2] for c in chunks)
    rows = chunks[0][0].shape[1]
    parts = [x for c in chunks for x in c]
    return pl.pallas_call(
        functools.partial(unpack_kernel, n, width, cuts),
        out_shape=[sds((1, rows, n * width))] * 3,
        in_specs=[SMEM] + [ANY] * len(parts),
        out_specs=[ANY] * 3,
        scratch_shapes=[pltpu.VMEM(x.shape[1:], BF) for x in parts for _ in range(3)]
        + [pltpu.SemaphoreType.DMA((3 * len(parts),))] * 2,
        compiler_params=params(60),
        cost_estimate=LONG,
        name="unpack",
    )(me, *parts)


def join_kernel(width, low_ref, *rest):
    m = (len(rest) - 3) // 2
    parts, out = rest[:m], rest[m]
    moves, col = [], 0
    for i, part in enumerate(parts):
        if i == m // 2:
            col = 0
        side = low_ref[0] if i < m // 2 else 1 - low_ref[0]
        start = pl.multiple_of(side * width + col, 128)
        col += part.shape[1]
        moves.append((part, out.at[0, :, pl.ds(start, part.shape[1])]))
    staged(moves, *rest[m + 1 :])


def join(low, own, pair):
    parts = own + pair
    rows = parts[0].shape[0]
    width = sum(x.shape[1] for x in own)
    return pl.pallas_call(
        functools.partial(join_kernel, width),
        out_shape=sds((1, rows, 2 * width)),
        in_specs=[SMEM] + [ANY] * len(parts),
        out_specs=ANY,
        scratch_shapes=[pltpu.VMEM(x.shape, BF) for x in parts]
        + [pltpu.SemaphoreType.DMA((len(parts),))] * 2,
        compiler_params=params(60),
        cost_estimate=LONG,
        name="join",
    )(low, *parts)


def place(block, me, per):
    return pl.multiple_of((((block // per) ^ me) * per + block % per) * BLK, BLK)


NT = (((1,), (1,)), ((), ()))
TN = (((0,), (0,)), ((), ()))


def dot(a, b, dims=(((1,), (0,)), ((), ()))):
    return lax.dot_general(a, b, dims, preferred_element_type=F32)


def soft_of(scores, axis):
    expo = jnp.exp(scores - jnp.max(scores, axis=axis, keepdims=True))
    return expo * (1.0 / jnp.sum(expo, axis=axis, keepdims=True))


def for_blocks(blocks, slots, nbr_ref, cnt_ref, body):
    def block(b, _):
        for count in range(1, slots + 1):

            @pl.when(cnt_ref[0, b] == count)
            def _():
                body(b, [nbr_ref[0, b, j] for j in range(count)])

        return 0

    lax.fori_loop(0, blocks, block, 0)


def gather(held, t, keys, per, out):
    for j, e in enumerate(keys):
        rows = pl.ds(pl.multiple_of(e % per * BLK, BLK), BLK)
        out[j * BLK : (j + 1) * BLK] = held[e // per, t, rows]


def fwd_kernel(heads, slots, scale, me_ref, nbr_ref, cnt_ref, held, attn_ref, swap_ref, t_ref, ks, vs):
    me = me_ref[0]
    n, per = held.shape[0], held.shape[2] // BLK

    def body(b, keys):
        here, there = place(b, me, per), place(b, me ^ 1, per)
        rows = pl.ds(pl.multiple_of(b % per * BLK, BLK), BLK)
        gather(held, 1, keys, per, ks)
        gather(held, 2, keys, per, vs)
        used = slice(0, len(keys) * BLK)
        cols = [slice(h * HD, (h + 1) * HD) for h in range(heads)]
        scores = [dot(held[b // per, 0, rows, c], ks[used, c], NT) * scale for c in cols]
        probs = [soft_of(x, 1).astype(BF) for x in scores]
        for c, p in zip(cols, probs):
            out = dot(p, vs[used, c]).astype(BF)
            attn_ref[pl.ds(here, BLK), c] = out
            swap_ref[pl.ds(there, BLK), c] = out

    for_blocks(n * per, slots, nbr_ref, cnt_ref, body)
    t_ref[...] = attn_ref[...].T


def attend(me, nbr, cnt, got, scale):
    n, _, rows, width = got.shape
    vm = pl.BlockSpec(memory_space=pltpu.VMEM)
    return pl.pallas_call(
        functools.partial(fwd_kernel, width // HD, nbr.shape[2], scale),
        out_shape=[sds((n * rows, width))] * 2 + [sds((width, n * rows))],
        in_specs=[SMEM] * 3 + [vm],
        out_specs=[vm] * 3,
        scratch_shapes=[pltpu.VMEM((nbr.shape[2] * BLK, width), BF)] * 2,
        compiler_params=params(60),
        cost_estimate=COST,
        name="attend",
    )(me, nbr, cnt, got)


def bwd_kernel(begin, slots, scale, me_ref, nbr_ref, cnt_ref, got_ref, *rest):
    d_refs, outs, (held, terms, dq, dk, dv, ks, vs, sem, d_sem) = rest[:4], rest[4:-9], rest[-9:]
    me = me_ref[0]
    n, _, rows, some = held.shape
    per = rows // BLK
    cols = pl.ds(begin, some)
    copies = [pltpu.make_async_copy(got_ref.at[:, :, :, cols], held, sem)]
    own_0, own_1, pair_0, pair_1 = d_refs
    for i, (ref, begin, end, t, start) in enumerate(
        (
            (own_0, 0, 3, 0, 0),
            (own_1, 0, 1, 0, 3),
            (pair_0, 0, 2, 1, 0),
            (pair_0, 2, 3, 1, 3),
            (pair_1, 0, 1, 1, 2),
        )
    ):
        part, there = pl.ds(begin * rows, (end - begin) * rows), pl.ds(start * rows, (end - begin) * rows)
        copies.append(
            pltpu.make_async_copy(ref.at[part, cols], terms.at[t, there], d_sem.at[i])
        )
    for c in copies:
        c.start()
    dk[...] = jnp.zeros_like(dk)
    dv[...] = jnp.zeros_like(dv)
    for c in copies:
        c.wait()

    def body(b, keys):
        here = pl.ds(place(b, me, per), BLK)
        rows_b = pl.ds(pl.multiple_of(b % per * BLK, BLK), BLK)
        gather(held, 1, keys, per, ks)
        gather(held, 2, keys, per, vs)
        used = slice(0, len(keys) * BLK)
        heads = [slice(h * HD, (h + 1) * HD) for h in range(some // HD)]
        qs = [held[b // per, 0, rows_b, c] for c in heads]
        ds = [
            (terms[0, here, c].astype(F32) + terms[1, here, c].astype(F32)).astype(BF)
            for c in heads
        ]
        softs = [soft_of(dot(ks[used, c], q, NT) * scale, 0) for c, q in zip(heads, qs)]
        dps = [dot(vs[used, c], d, NT) for c, d in zip(heads, ds)]
        dss = [
            (s * (p - jnp.sum(s * p, axis=0, keepdims=True))).astype(BF)
            for s, p in zip(softs, dps)
        ]
        for c, q, d, s, x in zip(heads, qs, ds, softs, dss):
            dq[b // per, rows_b, c] = (dot(x, ks[used, c], TN) * scale).astype(BF)
            to_v, to_k = dot(s.astype(BF), d), dot(x, q)
            for j, e in enumerate(keys):
                rows_e = pl.ds(pl.multiple_of(e * BLK, BLK), BLK)
                dv[rows_e, c] += to_v[j * BLK : (j + 1) * BLK]
                dk[rows_e, c] += to_k[j * BLK : (j + 1) * BLK]

    for_blocks(n * per, slots, nbr_ref, cnt_ref, body)
    for r, out in enumerate(outs):
        g = me ^ r
        rows_g = pl.ds(pl.multiple_of(g * rows, BLK), rows)
        out[0] = dq[g]
        out[1] = (dk[rows_g] * scale).astype(BF)
        out[2] = dv[rows_g].astype(BF)


def attend_back(me, nbr, cnt, got, terms, begin, end, scale):
    n, _, rows, _ = got.shape
    some = end - begin
    vm = pl.BlockSpec(memory_space=pltpu.VMEM)
    return pl.pallas_call(
        functools.partial(bwd_kernel, begin, nbr.shape[2], scale),
        out_shape=[sds((3, rows, some))] * n,
        in_specs=[SMEM] * 3 + [ANY] * 5,
        out_specs=[vm] * n,
        scratch_shapes=[
            pltpu.VMEM((n, 3, rows, some), BF),
            pltpu.VMEM((2, n * rows, some), BF),
            pltpu.VMEM((n, rows, some), BF),
            pltpu.VMEM((n * rows, some), F32),
            pltpu.VMEM((n * rows, some), F32),
            pltpu.VMEM((nbr.shape[2] * BLK, some), BF),
            pltpu.VMEM((nbr.shape[2] * BLK, some), BF),
            pltpu.SemaphoreType.DMA,
            pltpu.SemaphoreType.DMA((5,)),
        ],
        compiler_params=params(60),
        cost_estimate=COST,
        name="attend_back",
    )(me, nbr, cnt, got, *terms)


def project_kernel(a_ref, b_ref, wa_ref, wb_ref, *rest):
    y = dot(a_ref[...], wa_ref[...]) + dot(b_ref[...], wb_ref[...])
    if len(rest) == 1:
        rest[0][...] = y.astype(BF)
        return
    far_ref, own_ref, pair_ref = rest
    y = (y + far_ref[...].astype(F32)).astype(BF)
    rows = own_ref.shape[0]
    own_ref[...] = y[:rows]
    pair_ref[...] = y[rows:]


def project(a, b, wa, wb, begin, end, far=None, tile=512):
    rows, depth = a.shape
    rows //= 2
    cols = end - begin
    skip = begin // tile
    near = far is not None
    left = pl.BlockSpec((rows, depth), lambda j: (0 if near else 1, 0))
    right = pl.BlockSpec((depth, tile), lambda j: (0, skip + j))
    out = rows // 2 if near else rows
    return pl.pallas_call(
        project_kernel,
        grid=(cols // tile,),
        out_shape=[sds((out, cols))] * (2 if near else 1),
        in_specs=[left, left, right, right]
        + [pl.BlockSpec((rows, tile), lambda j: (0, j))] * int(near),
        out_specs=[pl.BlockSpec((out, tile), lambda j: (0, j))] * (2 if near else 1),
        compiler_params=params(60),
        cost_estimate=LONG if near else COST,
        name="project",
    )(a, b, wa, wb, *([far] if near else []))


def project_back_kernel(n, m, order, *refs):
    d_refs, w_refs, o_refs = refs[:n], refs[n : n + m], refs[n + m : n + 2 * m]
    held_d, held_w, sem = refs[n + 2 * m :]
    rows = d_refs[0].shape[0]
    copies = [
        pltpu.make_async_copy(d, held_d.at[pl.ds(i * rows, rows)], sem.at[i])
        for i, d in enumerate(d_refs)
    ] + [pltpu.make_async_copy(w, held_w.at[i], sem.at[n + i]) for i, w in enumerate(w_refs)]
    for c in copies:
        c.start()
    for c in copies[: n + 1]:
        c.wait()
    for i in range(m):
        if i:
            copies[n + i].wait()
        out = dot(held_d[...], held_w[i], NT).astype(BF)
        for r in range(n):
            there = order[i][r]
            o_refs[i][there * rows : (there + 1) * rows] = out[r * rows : (r + 1) * rows]


def project_back(ds, ws, order):
    n, m = len(ds), len(ws)
    rows, cols = ds[0].shape
    width = ws[0].shape[0]
    vm = pl.BlockSpec(memory_space=pltpu.VMEM)
    return pl.pallas_call(
        functools.partial(project_back_kernel, n, m, order),
        out_shape=[sds((n * rows, width))] * m,
        in_specs=[ANY] * (n + m),
        out_specs=[vm] * m,
        scratch_shapes=[
            pltpu.VMEM((n * rows, cols), BF),
            pltpu.VMEM((m, width, cols), BF),
            pltpu.SemaphoreType.DMA((n + m,)),
        ],
        compiler_params=params(60),
        cost_estimate=COST,
        name="project_back",
    )(*ds, *ws)


def weight_kernel(n, at, b_ref, *refs):
    ds, o_ref, bt, d = refs[:n], refs[n], refs[n + 1], refs[n + 2]
    rows = ds[0].shape[0]

    @pl.when(pl.program_id(0) == 0)
    def _():
        bt[...] = b_ref[...].T

    for r, piece in enumerate(ds):
        d[r * rows : (r + 1) * rows] = piece[...]
    for i, t in enumerate((at, bt)):
        out = dot(t[...], d[...]).astype(BF)
        o_ref[:, i] = out.reshape(o_ref.shape[0], *o_ref.shape[2:])


def weight_grad(at, b, ds, owners, tile=512):
    n = len(ds)
    tokens, width = b.shape
    rows, cols = ds[0].shape
    some = width // owners
    apart = owners if some % 16 == 0 else 1
    out = pl.pallas_call(
        functools.partial(weight_kernel, n),
        grid=(cols // tile,),
        out_shape=sds((apart, 2, width // apart, cols)),
        in_specs=[
            pl.BlockSpec((width, tokens), lambda j: (0, 0)),
            pl.BlockSpec((tokens, width), lambda j: (0, 0)),
        ]
        + [pl.BlockSpec((rows, tile), lambda j: (0, j))] * n,
        out_specs=pl.BlockSpec((apart, 2, width // apart, tile), lambda j: (0, 0, 0, j)),
        scratch_shapes=[pltpu.VMEM((width, tokens), BF), pltpu.VMEM((tokens, tile), BF)],
        compiler_params=params(60),
        cost_estimate=COST,
        name="weight_grad",
    )(at, b, *ds)
    if apart == 1:
        out = out.reshape(2, owners, some, cols).swapaxes(0, 1)
    return out.reshape(2 * width, cols)


def on_device(n, owners, q_proj, k_proj, v_proj, neighbours, counts, w_out, d_out):
    scale = 1.0 / math.sqrt(HD)
    seq = lax.axis_index("seq")
    me = seq.astype(jnp.int32)[None]
    half = d_out.shape[2] // 2
    low = seq & 1

    def to(x, r):
        return lax.ppermute(x, "seq", [(i, i ^ r) for i in range(n)])

    def mine(x):
        return lax.dynamic_slice_in_dim(x, low * half, half, 1)

    def theirs(x):
        return lax.dynamic_slice_in_dim(x, (1 - low) * half, half, 1)

    def after(x, *others):
        return lax.optimization_barrier((x, *others))[0]

    def exchange(x):
        return lax.all_to_all(x, "seq", split_axis=0, concat_axis=0, tiled=True)

    def exchange(x):
        return lax.all_to_all(x, "seq", split_axis=0, concat_axis=0, tiled=True)

    sent = pack(q_proj, k_proj, v_proj, n)
    got = exchange(sent)

    w_out = after(w_out, sent)
    w_a = lax.all_gather(mine(w_out), "zero", axis=0, tiled=True)
    d_local = after(d_out, sent)[0]
    d0, d_theirs = mine(d_local), theirs(d_local)

    w_pair = after(to(theirs(after(w_out, d0, d_theirs)), 1), w_a, got)
    w_b = lax.all_gather(w_pair, "zero", axis=0, tiled=True)

    d1 = to(d_theirs, 1)
    d2 = to(d0, 2)

    attn, swapped, attn_t = attend(me, neighbours, counts, got, scale)
    attn_pair = to(swapped, 1)
    d3 = to(after(d1, attn), 2)

    (own_0,) = project_back([d0, d1, d2], [w_a], ((0, 1, 2),))
    (sent_0,) = project_back([d0, after(d1, own_0), d2], [w_b], ((1, 0, 2),))
    pair_0 = to(sent_0, 1)
    attn_pair = after(attn_pair, sent_0)

    near_cut = half * 2 // 5
    ranges = [(0, near_cut), (near_cut, half)]
    far_0 = project(attn, attn_pair, w_a, w_b, *ranges[0])[0]
    (sent_1,) = project_back([after(d3, far_0)], [w_b], ((0,),))
    pair_1 = to(sent_1, 1)
    far_1 = project(attn, after(attn_pair, sent_1), w_a, w_b, *ranges[1])[0]
    after_far = after(attn_pair, far_1)
    y_far = [to(far_0, 2), to(far_1, 2)]
    (own_1,) = project_back([after(d3, after_far)], [w_a], ((0,),))

    gw = weight_grad(attn_t, after(after_far, own_1), [d0, d1, d2, d3], owners)

    terms = [own_0, after(own_1, gw), pair_0, pair_1]
    grads = attend_back(me, neighbours, counts, got, terms, 0, attn.shape[1], scale)
    back = [grads[0]] + [to(x, r) for r, x in enumerate(grads[1:], 1)]

    ys, y_pair, last = [], [], gw
    for c, far in zip(ranges, y_far):
        ys.append(project(after(attn, last), attn_pair, w_a, w_b, *c, far))
        y_pair.append(to(ys[-1][1], 1))
        last = y_pair[-1]
    y_own = [y[0] for y in ys]
    out_y = join(low.astype(jnp.int32)[None], y_own, y_pair)
    grad_q, grad_k, grad_v = unpack(me, [back])

    gw = lax.psum_scatter(after(gw, y_far[0], pair_0, pair_1), "zero", scatter_dimension=0, tiled=True)
    gw = after(gw, grads[0])
    rows = gw.shape[0] // 2
    gw_own, gw_pair = gw[:rows], to(gw[rows:], 1)
    grad_w = jnp.where(
        low == 0,
        jnp.concatenate([gw_own, gw_pair], axis=1),
        jnp.concatenate([gw_pair, gw_own], axis=1),
    ).astype(F32)
    return (out_y, grad_q, grad_k, grad_v, grad_w)


def solution(mesh):
    return jax.shard_map(
        functools.partial(on_device, mesh.shape["seq"], mesh.shape["zero"]),
        mesh=mesh,
        in_specs=(
            P("zero", "seq", None),
            P("zero", "seq", None),
            P("zero", "seq", None),
            P("zero", None, None),
            P("zero", None),
            P(("seq", "zero"), None),
            P("zero", "seq", None),
        ),
        out_specs=(
            P("zero", "seq", None),
            P("zero", "seq", None),
            P("zero", "seq", None),
            P("zero", "seq", None),
            P(("seq", "zero"), None),
        ),
        check_vma=False,
    )
```

```python
import functools
import math

import jax
import jax.numpy as jnp
from jax import lax
from jax.experimental import pallas as pl
from jax.experimental.pallas import tpu as pltpu
from jax.sharding import PartitionSpec as P

HD = 128
BLK = 128
MB = 1 << 20
BF = jnp.bfloat16
COST = pl.CostEstimate(flops=1024, bytes_accessed=1024, transcendentals=0)
LONG = pl.CostEstimate(flops=1024, bytes_accessed=1024, transcendentals=0)
F32 = jnp.float32


ANY = pl.BlockSpec(memory_space=pl.ANY)
SMEM = pl.BlockSpec(memory_space=pltpu.SMEM)


def params(mb):
    return pltpu.CompilerParams(vmem_limit_bytes=mb * MB)


def sds(shape, dtype=BF):
    return jax.ShapeDtypeStruct(shape, dtype)


def run_copies(copies):
    for c in copies:
        c.start()
    for c in copies:
        c.wait()


def staged(moves, *rest):
    held, sem_in, sem_out = rest[:-2], rest[-2], rest[-1]
    ins = [pltpu.make_async_copy(a, h, sem_in.at[i]) for i, ((a, _), h) in enumerate(zip(moves, held))]
    outs = [pltpu.make_async_copy(h, b, sem_out.at[i]) for i, ((_, b), h) in enumerate(zip(moves, held))]
    for c in ins:
        c.start()
    for c, o in zip(ins, outs):
        c.wait()
        o.start()
    for o in outs:
        o.wait()


def pack_kernel(q_ref, k_ref, v_ref, out_ref, *rest):
    n, _, _, width = out_ref.shape
    moves = [
        (src.at[0, :, pl.ds(g * width, width)], out_ref.at[g, t])
        for g in range(n)
        for t, src in enumerate((q_ref, k_ref, v_ref))
    ]
    staged(moves, *rest)


def pack(q, k, v, n):
    rows, cols = q.shape[1:]
    width = cols // n
    return pl.pallas_call(
        pack_kernel,
        out_shape=sds((n, 3, rows, width)),
        in_specs=[ANY, ANY, ANY],
        out_specs=ANY,
        scratch_shapes=[pltpu.VMEM((rows, width), BF)] * (3 * n)
        + [pltpu.SemaphoreType.DMA((3 * n,))] * 2,
        compiler_params=params(64),
        cost_estimate=COST,
        name="pack",
    )(q, k, v)


def unpack_kernel(n, width, cuts, me_ref, *rest):
    m = n * len(cuts)
    parts, outs = rest[:m], rest[m : m + 3]
    moves = []
    for i, part in enumerate(parts):
        col = pl.multiple_of((me_ref[0] ^ (i % n)) * width + cuts[i // n], 128)
        for t in range(3):
            moves.append((part.at[t], outs[t].at[0, :, pl.ds(col, part.shape[2])]))
    staged(moves, *rest[m + 3 :])


def unpack(me, chunks):
    n = len(chunks[0])
    cuts = [sum(c[0].shape[2] for c in chunks[:i]) for i in range(len(chunks))]
    width = sum(c[0].shape[2] for c in chunks)
    rows = chunks[0][0].shape[1]
    parts = [x for c in chunks for x in c]
    return pl.pallas_call(
        functools.partial(unpack_kernel, n, width, cuts),
        out_shape=[sds((1, rows, n * width))] * 3,
        in_specs=[SMEM] + [ANY] * len(parts),
        out_specs=[ANY] * 3,
        scratch_shapes=[pltpu.VMEM(x.shape[1:], BF) for x in parts for _ in range(3)]
        + [pltpu.SemaphoreType.DMA((3 * len(parts),))] * 2,
        compiler_params=params(64),
        cost_estimate=LONG,
        name="unpack",
    )(me, *parts)


def join_kernel(width, low_ref, *rest):
    m = (len(rest) - 3) // 2
    parts, out = rest[:m], rest[m]
    moves, col = [], 0
    for i, part in enumerate(parts):
        if i == m // 2:
            col = 0
        side = low_ref[0] if i < m // 2 else 1 - low_ref[0]
        start = pl.multiple_of(side * width + col, 128)
        col += part.shape[1]
        moves.append((part, out.at[0, :, pl.ds(start, part.shape[1])]))
    staged(moves, *rest[m + 1 :])


def join(low, own, pair):
    parts = own + pair
    rows = parts[0].shape[0]
    width = sum(x.shape[1] for x in own)
    return pl.pallas_call(
        functools.partial(join_kernel, width),
        out_shape=sds((1, rows, 2 * width)),
        in_specs=[SMEM] + [ANY] * len(parts),
        out_specs=ANY,
        scratch_shapes=[pltpu.VMEM(x.shape, BF) for x in parts]
        + [pltpu.SemaphoreType.DMA((len(parts),))] * 2,
        compiler_params=params(64),
        cost_estimate=LONG,
        name="join",
    )(low, *parts)


def place(block, me, per):
    return pl.multiple_of((((block // per) ^ me) * per + block % per) * BLK, BLK)


NT = (((1,), (1,)), ((), ()))
TN = (((0,), (0,)), ((), ()))


def dot(a, b, dims=(((1,), (0,)), ((), ()))):
    return lax.dot_general(a, b, dims, preferred_element_type=F32)


def soft_of(scores, axis):
    expo = jnp.exp(scores - jnp.max(scores, axis=axis, keepdims=True))
    return expo * (1.0 / jnp.sum(expo, axis=axis, keepdims=True))


def for_blocks(blocks, slots, nbr_ref, cnt_ref, body):
    def block(b, _):
        for count in range(1, slots + 1):

            @pl.when(cnt_ref[0, b] == count)
            def _():
                body(b, [nbr_ref[0, b, j] for j in range(count)])

        return 0

    lax.fori_loop(0, blocks, block, 0)


def gather(held, t, keys, per, out):
    for j, e in enumerate(keys):
        rows = pl.ds(pl.multiple_of(e % per * BLK, BLK), BLK)
        out[j * BLK : (j + 1) * BLK] = held[e // per, t, rows]


def fwd_kernel(heads, slots, scale, me_ref, nbr_ref, cnt_ref, held, attn_ref, swap_ref, t_ref, ks, vs):
    me = me_ref[0]
    n, per = held.shape[0], held.shape[2] // BLK

    def body(b, keys):
        here, there = place(b, me, per), place(b, me ^ 1, per)
        rows = pl.ds(pl.multiple_of(b % per * BLK, BLK), BLK)
        gather(held, 1, keys, per, ks)
        gather(held, 2, keys, per, vs)
        used = slice(0, len(keys) * BLK)
        cols = [slice(h * HD, (h + 1) * HD) for h in range(heads)]
        scores = [dot(held[b // per, 0, rows, c], ks[used, c], NT) * scale for c in cols]
        probs = [soft_of(x, 1).astype(BF) for x in scores]
        for c, p in zip(cols, probs):
            out = dot(p, vs[used, c]).astype(BF)
            attn_ref[pl.ds(here, BLK), c] = out
            swap_ref[pl.ds(there, BLK), c] = out

    for_blocks(n * per, slots, nbr_ref, cnt_ref, body)
    t_ref[...] = attn_ref[...].T


def attend(me, nbr, cnt, got, scale):
    n, _, rows, width = got.shape
    vm = pl.BlockSpec(memory_space=pltpu.VMEM)
    return pl.pallas_call(
        functools.partial(fwd_kernel, width // HD, nbr.shape[2], scale),
        out_shape=[sds((n * rows, width))] * 2 + [sds((width, n * rows))],
        in_specs=[SMEM] * 3 + [vm],
        out_specs=[vm] * 3,
        scratch_shapes=[pltpu.VMEM((nbr.shape[2] * BLK, width), BF)] * 2,
        compiler_params=params(64),
        cost_estimate=COST,
        name="attend",
    )(me, nbr, cnt, got)


def bwd_kernel(begin, slots, scale, me_ref, nbr_ref, cnt_ref, got_ref, *rest):
    d_refs, outs, (held, terms, dq, dk, dv, ks, vs, sem, d_sem) = rest[:4], rest[4:-9], rest[-9:]
    me = me_ref[0]
    n, _, rows, some = held.shape
    per = rows // BLK
    cols = pl.ds(begin, some)
    copies = [pltpu.make_async_copy(got_ref.at[:, :, :, cols], held, sem)]
    own_0, own_1, pair_0, pair_1 = d_refs
    for i, (ref, begin, end, t, start) in enumerate(
        (
            (own_0, 0, 3, 0, 0),
            (own_1, 0, 1, 0, 3),
            (pair_0, 0, 2, 1, 0),
            (pair_0, 2, 3, 1, 3),
            (pair_1, 0, 1, 1, 2),
        )
    ):
        part, there = pl.ds(begin * rows, (end - begin) * rows), pl.ds(start * rows, (end - begin) * rows)
        copies.append(
            pltpu.make_async_copy(ref.at[part, cols], terms.at[t, there], d_sem.at[i])
        )
    for c in copies:
        c.start()
    dk[...] = jnp.zeros_like(dk)
    dv[...] = jnp.zeros_like(dv)
    for c in copies:
        c.wait()

    def body(b, keys):
        here = pl.ds(place(b, me, per), BLK)
        rows_b = pl.ds(pl.multiple_of(b % per * BLK, BLK), BLK)
        gather(held, 1, keys, per, ks)
        gather(held, 2, keys, per, vs)
        used = slice(0, len(keys) * BLK)
        heads = [slice(h * HD, (h + 1) * HD) for h in range(some // HD)]
        qs = [held[b // per, 0, rows_b, c] for c in heads]
        ds = [
            (terms[0, here, c].astype(F32) + terms[1, here, c].astype(F32)).astype(BF)
            for c in heads
        ]
        softs = [soft_of(dot(ks[used, c], q, NT) * scale, 0) for c, q in zip(heads, qs)]
        dps = [dot(vs[used, c], d, NT) for c, d in zip(heads, ds)]
        dss = [
            (s * (p - jnp.sum(s * p, axis=0, keepdims=True))).astype(BF)
            for s, p in zip(softs, dps)
        ]
        for c, q, d, s, x in zip(heads, qs, ds, softs, dss):
            dq[b // per, rows_b, c] = (dot(x, ks[used, c], TN) * scale).astype(BF)
            to_v, to_k = dot(s.astype(BF), d), dot(x, q)
            for j, e in enumerate(keys):
                rows_e = pl.ds(pl.multiple_of(e * BLK, BLK), BLK)
                dv[rows_e, c] += to_v[j * BLK : (j + 1) * BLK]
                dk[rows_e, c] += to_k[j * BLK : (j + 1) * BLK]

    for_blocks(n * per, slots, nbr_ref, cnt_ref, body)
    for r, out in enumerate(outs):
        g = me ^ r
        rows_g = pl.ds(pl.multiple_of(g * rows, BLK), rows)
        out[0] = dq[g]
        out[1] = (dk[rows_g] * scale).astype(BF)
        out[2] = dv[rows_g].astype(BF)


def attend_back(me, nbr, cnt, got, terms, begin, end, scale):
    n, _, rows, _ = got.shape
    some = end - begin
    vm = pl.BlockSpec(memory_space=pltpu.VMEM)
    return pl.pallas_call(
        functools.partial(bwd_kernel, begin, nbr.shape[2], scale),
        out_shape=[sds((3, rows, some))] * n,
        in_specs=[SMEM] * 3 + [ANY] * 5,
        out_specs=[vm] * n,
        scratch_shapes=[
            pltpu.VMEM((n, 3, rows, some), BF),
            pltpu.VMEM((2, n * rows, some), BF),
            pltpu.VMEM((n, rows, some), BF),
            pltpu.VMEM((n * rows, some), F32),
            pltpu.VMEM((n * rows, some), F32),
            pltpu.VMEM((nbr.shape[2] * BLK, some), BF),
            pltpu.VMEM((nbr.shape[2] * BLK, some), BF),
            pltpu.SemaphoreType.DMA,
            pltpu.SemaphoreType.DMA((5,)),
        ],
        compiler_params=params(64),
        cost_estimate=COST,
        name="attend_back",
    )(me, nbr, cnt, got, *terms)


def project_own_kernel(a_ref, w_ref, o_ref):
    o_ref[...] = dot(a_ref[...], w_ref[...])


def project_own(a, w, tile=512):
    rows, depth = a.shape
    cols = w.shape[1]
    return pl.pallas_call(
        project_own_kernel,
        grid=(cols // tile,),
        out_shape=sds((rows, cols), F32),
        in_specs=[
            pl.BlockSpec((rows, depth), lambda j: (0, 0)),
            pl.BlockSpec((depth, tile), lambda j: (0, j)),
        ],
        out_specs=pl.BlockSpec((rows, tile), lambda j: (0, j)),
        compiler_params=params(64),
        cost_estimate=COST,
        name="project_own",
    )(a, w)


def project_kernel(own_ref, b_ref, w_ref, *rest):
    y = own_ref[...] + dot(b_ref[...], w_ref[...])
    if len(rest) == 1:
        rest[0][...] = y.astype(BF)
        return
    far_ref, own_out, pair_out = rest
    y = (y + far_ref[...].astype(F32)).astype(BF)
    rows = own_out.shape[0]
    own_out[...] = y[:rows]
    pair_out[...] = y[rows:]


def project(own, b, w, begin, end, far=None, tile=512):
    rows, depth = b.shape
    rows //= 2
    cols = end - begin
    skip = begin // tile
    near = far is not None
    half = 0 if near else 1
    out = rows // 2 if near else rows
    return pl.pallas_call(
        project_kernel,
        grid=(cols // tile,),
        out_shape=[sds((out, cols))] * (2 if near else 1),
        in_specs=[
            pl.BlockSpec((rows, tile), lambda j: (half, skip + j)),
            pl.BlockSpec((rows, depth), lambda j: (half, 0)),
            pl.BlockSpec((depth, tile), lambda j: (0, skip + j)),
        ]
        + [pl.BlockSpec((rows, tile), lambda j: (0, j))] * int(near),
        out_specs=[pl.BlockSpec((out, tile), lambda j: (0, j))] * (2 if near else 1),
        compiler_params=params(64),
        cost_estimate=LONG if near else COST,
        name="project",
    )(own, b, w, *([far] if near else []))


def project_back_kernel(n, m, order, *refs):
    d_refs, w_refs, o_refs = refs[:n], refs[n : n + m], refs[n + m : n + 2 * m]
    held_d, held_w, sem = refs[n + 2 * m :]
    rows = d_refs[0].shape[0]
    copies = [
        pltpu.make_async_copy(d, held_d.at[pl.ds(i * rows, rows)], sem.at[i])
        for i, d in enumerate(d_refs)
    ] + [pltpu.make_async_copy(w, held_w.at[i], sem.at[n + i]) for i, w in enumerate(w_refs)]
    for c in copies:
        c.start()
    for c in copies[: n + 1]:
        c.wait()
    for i in range(m):
        if i:
            copies[n + i].wait()
        out = dot(held_d[...], held_w[i], NT).astype(BF)
        for r in range(n):
            there = order[i][r]
            o_refs[i][there * rows : (there + 1) * rows] = out[r * rows : (r + 1) * rows]


def project_back(ds, ws, order):
    n, m = len(ds), len(ws)
    rows, cols = ds[0].shape
    width = ws[0].shape[0]
    vm = pl.BlockSpec(memory_space=pltpu.VMEM)
    return pl.pallas_call(
        functools.partial(project_back_kernel, n, m, order),
        out_shape=[sds((n * rows, width))] * m,
        in_specs=[ANY] * (n + m),
        out_specs=[vm] * m,
        scratch_shapes=[
            pltpu.VMEM((n * rows, cols), BF),
            pltpu.VMEM((m, width, cols), BF),
            pltpu.SemaphoreType.DMA((n + m,)),
        ],
        compiler_params=params(64),
        cost_estimate=COST,
        name="project_back",
    )(*ds, *ws)


def weight_own_kernel(n, at, *refs):
    ds, o_ref, d = refs[:n], refs[n], refs[n + 1]
    rows = ds[0].shape[0]
    for r, piece in enumerate(ds):
        d[r * rows : (r + 1) * rows] = piece[...]
    o_ref[...] = dot(at[...], d[...])


def weight_own(at, ds, tile=512):
    n = len(ds)
    width = at.shape[0]
    rows, cols = ds[0].shape
    return pl.pallas_call(
        functools.partial(weight_own_kernel, n),
        grid=(cols // tile,),
        out_shape=sds((width, cols), F32),
        in_specs=[pl.BlockSpec((width, n * rows), lambda j: (0, 0))]
        + [pl.BlockSpec((rows, tile), lambda j: (0, j))] * n,
        out_specs=pl.BlockSpec((width, tile), lambda j: (0, j)),
        scratch_shapes=[pltpu.VMEM((n * rows, tile), BF)],
        compiler_params=params(64),
        cost_estimate=COST,
        name="weight_own",
    )(at, *ds)


def weight_kernel(n, done_ref, at, b_ref, *refs):
    ds, o_ref, bt, d = refs[:n], refs[n], refs[n + 1], refs[n + 2]
    rows = ds[0].shape[0]

    @pl.when(pl.program_id(0) == 0)
    def _():
        bt[...] = b_ref[...].T

    for r, piece in enumerate(ds):
        d[r * rows : (r + 1) * rows] = piece[...]
    own = done_ref[...] + dot(at[...], ds[n - 1][...])
    for i, out in enumerate((own, dot(bt[...], d[...]))):
        o_ref[:, i] = out.astype(BF).reshape(o_ref.shape[0], *o_ref.shape[2:])


def weight_grad(done, at, b, ds, owners, tile=512):
    n = len(ds)
    tokens, width = b.shape
    rows, cols = ds[0].shape
    some = width // owners
    apart = owners if some % 16 == 0 else 1
    out = pl.pallas_call(
        functools.partial(weight_kernel, n),
        grid=(cols // tile,),
        out_shape=sds((apart, 2, width // apart, cols)),
        in_specs=[
            pl.BlockSpec((width, tile), lambda j: (0, j)),
            pl.BlockSpec((width, rows), lambda j: (0, n - 1)),
            pl.BlockSpec((tokens, width), lambda j: (0, 0)),
        ]
        + [pl.BlockSpec((rows, tile), lambda j: (0, j))] * n,
        out_specs=pl.BlockSpec((apart, 2, width // apart, tile), lambda j: (0, 0, 0, j)),
        scratch_shapes=[pltpu.VMEM((width, tokens), BF), pltpu.VMEM((tokens, tile), BF)],
        compiler_params=params(64),
        cost_estimate=COST,
        name="weight_grad",
    )(done, at, b, *ds)
    if apart == 1:
        out = out.reshape(2, owners, some, cols).swapaxes(0, 1)
    return out.reshape(2 * width, cols)


def on_device(n, owners, q_proj, k_proj, v_proj, neighbours, counts, w_out, d_out):
    scale = 1.0 / math.sqrt(HD)
    seq = lax.axis_index("seq")
    me = seq.astype(jnp.int32)[None]
    half = d_out.shape[2] // 2
    low = seq & 1

    def to(x, r):
        return lax.ppermute(x, "seq", [(i, i ^ r) for i in range(n)])

    def mine(x):
        return lax.dynamic_slice_in_dim(x, low * half, half, 1)

    def theirs(x):
        return lax.dynamic_slice_in_dim(x, (1 - low) * half, half, 1)

    def after(x, *others):
        return lax.optimization_barrier((x, *others))[0]

    def exchange(x):
        return lax.all_to_all(x, "seq", split_axis=0, concat_axis=0, tiled=True)

    def exchange(x):
        return lax.all_to_all(x, "seq", split_axis=0, concat_axis=0, tiled=True)

    sent = pack(q_proj, k_proj, v_proj, n)
    got = exchange(sent)

    w_out = after(w_out, sent)
    w_a = lax.all_gather(mine(w_out), "zero", axis=0, tiled=True)
    d_local = after(d_out, sent)[0]
    d0, d_theirs = mine(d_local), theirs(d_local)

    w_pair = after(to(theirs(after(w_out, d0, d_theirs)), 1), w_a, got)
    w_b = lax.all_gather(w_pair, "zero", axis=0, tiled=True)

    d1 = to(d_theirs, 1)
    d2 = to(d0, 2)

    attn, swapped, attn_t = attend(me, neighbours, counts, got, scale)
    attn_pair = to(swapped, 1)
    y_own = project_own(after(attn, swapped), w_a)
    d3 = to(after(d1, y_own), 2)

    (own_0,) = project_back([d0, d1, d2], [w_a], ((0, 1, 2),))
    (sent_0,) = project_back([d0, after(d1, own_0), d2], [w_b], ((1, 0, 2),))
    pair_0 = to(sent_0, 1)
    gw_own = weight_own(after(attn_t, sent_0), [d0, d1, d2])
    attn_pair = after(attn_pair, gw_own)

    near_cut = half * 2 // 5
    ranges = [(0, near_cut), (near_cut, half)]
    far_0 = project(y_own, attn_pair, w_b, *ranges[0])[0]
    (sent_1,) = project_back([after(d3, far_0)], [w_b], ((0,),))
    pair_1 = to(sent_1, 1)
    far_1 = project(y_own, after(attn_pair, sent_1), w_b, *ranges[1])[0]
    after_far = after(attn_pair, far_1)
    y_far = [to(far_0, 2), to(far_1, 2)]
    (own_1,) = project_back([after(d3, after_far)], [w_a], ((0,),))

    gw = weight_grad(gw_own, attn_t, after(after_far, own_1), [d0, d1, d2, d3], owners)

    terms = [own_0, after(own_1, gw), pair_0, pair_1]
    grads = attend_back(me, neighbours, counts, got, terms, 0, attn.shape[1], scale)
    back = [grads[0]] + [to(x, r) for r, x in enumerate(grads[1:], 1)]

    ys, y_pair, last = [], [], gw
    for c, far in zip(ranges, y_far):
        ys.append(project(y_own, after(attn_pair, last), w_b, *c, far))
        y_pair.append(to(ys[-1][1], 1))
        last = y_pair[-1]
    out_y = join(low.astype(jnp.int32)[None], [y[0] for y in ys], y_pair)
    grad_q, grad_k, grad_v = unpack(me, [back])

    gw = lax.psum_scatter(after(gw, y_far[0], pair_0, pair_1), "zero", scatter_dimension=0, tiled=True)
    gw = after(gw, grads[0])
    rows = gw.shape[0] // 2
    gw_own, gw_pair = gw[:rows], to(gw[rows:], 1)
    grad_w = jnp.where(
        low == 0,
        jnp.concatenate([gw_own, gw_pair], axis=1),
        jnp.concatenate([gw_pair, gw_own], axis=1),
    ).astype(F32)
    return (out_y, grad_q, grad_k, grad_v, grad_w)


def solution(mesh):
    return jax.shard_map(
        functools.partial(on_device, mesh.shape["seq"], mesh.shape["zero"]),
        mesh=mesh,
        in_specs=(
            P("zero", "seq", None),
            P("zero", "seq", None),
            P("zero", "seq", None),
            P("zero", None, None),
            P("zero", None),
            P(("seq", "zero"), None),
            P("zero", "seq", None),
        ),
        out_specs=(
            P("zero", "seq", None),
            P("zero", "seq", None),
            P("zero", "seq", None),
            P("zero", "seq", None),
            P(("seq", "zero"), None),
        ),
        check_vma=False,
    )
```

```python
import functools
import math

import jax
import jax.numpy as jnp
from jax import lax
from jax.experimental import pallas as pl
from jax.experimental.pallas import tpu as pltpu
from jax.sharding import PartitionSpec as P

HD = 128
BLK = 128
MB = 1 << 20
BF = jnp.bfloat16
COST = pl.CostEstimate(flops=1024, bytes_accessed=1024, transcendentals=0)
LONG = pl.CostEstimate(flops=1024, bytes_accessed=1024, transcendentals=0)
F32 = jnp.float32


ANY = pl.BlockSpec(memory_space=pl.ANY)
SMEM = pl.BlockSpec(memory_space=pltpu.SMEM)


def params(mb):
    return pltpu.CompilerParams(vmem_limit_bytes=mb * MB)


def sds(shape, dtype=BF):
    return jax.ShapeDtypeStruct(shape, dtype)


def run_copies(copies):
    for c in copies:
        c.start()
    for c in copies:
        c.wait()


def staged(moves, *rest):
    held, sem_in, sem_out = rest[:-2], rest[-2], rest[-1]
    ins = [pltpu.make_async_copy(a, h, sem_in.at[i]) for i, ((a, _), h) in enumerate(zip(moves, held))]
    outs = [pltpu.make_async_copy(h, b, sem_out.at[i]) for i, ((_, b), h) in enumerate(zip(moves, held))]
    for c in ins:
        c.start()
    for c, o in zip(ins, outs):
        c.wait()
        o.start()
    for o in outs:
        o.wait()


def pack_kernel(n, width, me_ref, q_ref, k_ref, v_ref, *rest):
    outs = rest[: n - 1]
    moves = []
    for r, out in enumerate(outs, 1):
        col = pl.multiple_of((me_ref[0] ^ r) * width, 128)
        for t, src in enumerate((q_ref, k_ref, v_ref)):
            moves.append((src.at[0, :, pl.ds(col, width)], out.at[t]))
    staged(moves, *rest[n - 1 :])


def pack(me, q, k, v, n):
    rows, cols = q.shape[1:]
    width = cols // n
    return pl.pallas_call(
        functools.partial(pack_kernel, n, width),
        out_shape=[sds((3, rows, width))] * (n - 1),
        in_specs=[SMEM, ANY, ANY, ANY],
        out_specs=[ANY] * (n - 1),
        scratch_shapes=[pltpu.VMEM((rows, width), BF)] * (3 * (n - 1))
        + [pltpu.SemaphoreType.DMA((3 * (n - 1),))] * 2,
        compiler_params=params(64),
        cost_estimate=COST,
        name="pack",
    )(me, q, k, v)


def load_copies(me, own, parts, held, sem):
    width = held.shape[3]
    col = pl.multiple_of(me * width, 128)
    copies = [
        pltpu.make_async_copy(x.at[0, :, pl.ds(col, width)], held.at[me, t], sem.at[t])
        for t, x in enumerate(own)
    ]
    for r, part in enumerate(parts, 1):
        copies.append(pltpu.make_async_copy(part, held.at[me ^ r], sem.at[2 + r]))
    return copies


def unpack_kernel(n, width, cuts, me_ref, *rest):
    m = n * len(cuts)
    parts, outs = rest[:m], rest[m : m + 3]
    moves = []
    for i, part in enumerate(parts):
        col = pl.multiple_of((me_ref[0] ^ (i % n)) * width + cuts[i // n], 128)
        for t in range(3):
            moves.append((part.at[t], outs[t].at[0, :, pl.ds(col, part.shape[2])]))
    staged(moves, *rest[m + 3 :])


def unpack(me, chunks):
    n = len(chunks[0])
    cuts = [sum(c[0].shape[2] for c in chunks[:i]) for i in range(len(chunks))]
    width = sum(c[0].shape[2] for c in chunks)
    rows = chunks[0][0].shape[1]
    parts = [x for c in chunks for x in c]
    return pl.pallas_call(
        functools.partial(unpack_kernel, n, width, cuts),
        out_shape=[sds((1, rows, n * width))] * 3,
        in_specs=[SMEM] + [ANY] * len(parts),
        out_specs=[ANY] * 3,
        scratch_shapes=[pltpu.VMEM(x.shape[1:], BF) for x in parts for _ in range(3)]
        + [pltpu.SemaphoreType.DMA((3 * len(parts),))] * 2,
        compiler_params=params(64),
        cost_estimate=LONG,
        name="unpack",
    )(me, *parts)


def join_kernel(width, low_ref, *rest):
    m = (len(rest) - 3) // 2
    parts, out = rest[:m], rest[m]
    moves, col = [], 0
    for i, part in enumerate(parts):
        if i == m // 2:
            col = 0
        side = low_ref[0] if i < m // 2 else 1 - low_ref[0]
        start = pl.multiple_of(side * width + col, 128)
        col += part.shape[1]
        moves.append((part, out.at[0, :, pl.ds(start, part.shape[1])]))
    staged(moves, *rest[m + 1 :])


def join(low, own, pair):
    parts = own + pair
    rows = parts[0].shape[0]
    width = sum(x.shape[1] for x in own)
    return pl.pallas_call(
        functools.partial(join_kernel, width),
        out_shape=sds((1, rows, 2 * width)),
        in_specs=[SMEM] + [ANY] * len(parts),
        out_specs=ANY,
        scratch_shapes=[pltpu.VMEM(x.shape, BF) for x in parts]
        + [pltpu.SemaphoreType.DMA((len(parts),))] * 2,
        compiler_params=params(64),
        cost_estimate=LONG,
        name="join",
    )(low, *parts)


def place(block, me, per):
    return pl.multiple_of((((block // per) ^ me) * per + block % per) * BLK, BLK)


NT = (((1,), (1,)), ((), ()))
TN = (((0,), (0,)), ((), ()))


def dot(a, b, dims=(((1,), (0,)), ((), ()))):
    return lax.dot_general(a, b, dims, preferred_element_type=F32)


def soft_of(scores, axis):
    expo = jnp.exp(scores - jnp.max(scores, axis=axis, keepdims=True))
    return expo * (1.0 / jnp.sum(expo, axis=axis, keepdims=True))


def for_blocks(blocks, slots, nbr_ref, cnt_ref, body):
    def block(b, _):
        for count in range(1, slots + 1):

            @pl.when(cnt_ref[0, b] == count)
            def _():
                body(b, [nbr_ref[0, b, j] for j in range(count)])

        return 0

    lax.fori_loop(0, blocks, block, 0)


def gather(held, t, keys, per, out):
    for j, e in enumerate(keys):
        rows = pl.ds(pl.multiple_of(e % per * BLK, BLK), BLK)
        out[j * BLK : (j + 1) * BLK] = held[e // per, t, rows]


def fwd_kernel(heads, slots, scale, me_ref, nbr_ref, cnt_ref, *rest):
    own, parts, (attn_ref, swap_ref, t_ref, held, ks, vs, sem) = rest[:3], rest[3:-7], rest[-7:]
    me = me_ref[0]
    run_copies(load_copies(me, own, parts, held, sem))
    n, per = held.shape[0], held.shape[2] // BLK

    def body(b, keys):
        here, there = place(b, me, per), place(b, me ^ 1, per)
        rows = pl.ds(pl.multiple_of(b % per * BLK, BLK), BLK)
        gather(held, 1, keys, per, ks)
        gather(held, 2, keys, per, vs)
        used = slice(0, len(keys) * BLK)
        cols = [slice(h * HD, (h + 1) * HD) for h in range(heads)]
        scores = [dot(held[b // per, 0, rows, c], ks[used, c], NT) * scale for c in cols]
        probs = [soft_of(x, 1).astype(BF) for x in scores]
        for c, p in zip(cols, probs):
            out = dot(p, vs[used, c]).astype(BF)
            attn_ref[pl.ds(here, BLK), c] = out
            swap_ref[pl.ds(there, BLK), c] = out

    for_blocks(n * per, slots, nbr_ref, cnt_ref, body)
    t_ref[...] = attn_ref[...].T


def attend(me, nbr, cnt, got, scale):
    n = len(got) - 2
    _, rows, width = got[3].shape
    vm = pl.BlockSpec(memory_space=pltpu.VMEM)
    return pl.pallas_call(
        functools.partial(fwd_kernel, width // HD, nbr.shape[2], scale),
        out_shape=[sds((n * rows, width))] * 2 + [sds((width, n * rows))],
        in_specs=[SMEM] * 3 + [ANY] * len(got),
        out_specs=[vm] * 3,
        scratch_shapes=[pltpu.VMEM((n, 3, rows, width), BF)]
        + [pltpu.VMEM((nbr.shape[2] * BLK, width), BF)] * 2
        + [pltpu.SemaphoreType.DMA((n + 2,))],
        compiler_params=params(64),
        cost_estimate=COST,
        name="attend",
    )(me, nbr, cnt, *got)


def bwd_kernel(n_got, slots, scale, me_ref, nbr_ref, cnt_ref, *rest):
    got, rest = rest[:n_got], rest[n_got:]
    d_refs, outs, (held, terms, dq, dk, dv, ks, vs, sem, d_sem) = rest[:4], rest[4:-9], rest[-9:]
    me = me_ref[0]
    n, _, rows, some = held.shape
    per = rows // BLK
    copies = load_copies(me, got[:3], got[3:], held, sem)
    own_0, own_1, pair_0, pair_1 = d_refs
    for i, (ref, begin, end, t, start) in enumerate(
        (
            (own_0, 0, 3, 0, 0),
            (own_1, 0, 1, 0, 3),
            (pair_0, 0, 2, 1, 0),
            (pair_0, 2, 3, 1, 3),
            (pair_1, 0, 1, 1, 2),
        )
    ):
        part, there = pl.ds(begin * rows, (end - begin) * rows), pl.ds(start * rows, (end - begin) * rows)
        copies.append(
            pltpu.make_async_copy(ref.at[part], terms.at[t, there], d_sem.at[i])
        )
    for c in copies:
        c.start()
    dk[...] = jnp.zeros_like(dk)
    dv[...] = jnp.zeros_like(dv)
    for c in copies:
        c.wait()

    def body(b, keys):
        here = pl.ds(place(b, me, per), BLK)
        rows_b = pl.ds(pl.multiple_of(b % per * BLK, BLK), BLK)
        gather(held, 1, keys, per, ks)
        gather(held, 2, keys, per, vs)
        used = slice(0, len(keys) * BLK)
        heads = [slice(h * HD, (h + 1) * HD) for h in range(some // HD)]
        qs = [held[b // per, 0, rows_b, c] for c in heads]
        ds = [
            (terms[0, here, c].astype(F32) + terms[1, here, c].astype(F32)).astype(BF)
            for c in heads
        ]
        softs = [soft_of(dot(ks[used, c], q, NT) * scale, 0) for c, q in zip(heads, qs)]
        dps = [dot(vs[used, c], d, NT) for c, d in zip(heads, ds)]
        dss = [
            (s * (p - jnp.sum(s * p, axis=0, keepdims=True))).astype(BF)
            for s, p in zip(softs, dps)
        ]
        for c, q, d, s, x in zip(heads, qs, ds, softs, dss):
            dq[b // per, rows_b, c] = (dot(x, ks[used, c], TN) * scale).astype(BF)
            to_v, to_k = dot(s.astype(BF), d), dot(x, q)
            for j, e in enumerate(keys):
                rows_e = pl.ds(pl.multiple_of(e * BLK, BLK), BLK)
                dv[rows_e, c] += to_v[j * BLK : (j + 1) * BLK]
                dk[rows_e, c] += to_k[j * BLK : (j + 1) * BLK]

    for_blocks(n * per, slots, nbr_ref, cnt_ref, body)
    for r, out in enumerate(outs):
        g = me ^ r
        rows_g = pl.ds(pl.multiple_of(g * rows, BLK), rows)
        out[0] = dq[g]
        out[1] = (dk[rows_g] * scale).astype(BF)
        out[2] = dv[rows_g].astype(BF)


def attend_back(me, nbr, cnt, got, terms, scale):
    n = len(got) - 2
    _, rows, some = got[3].shape
    vm = pl.BlockSpec(memory_space=pltpu.VMEM)
    return pl.pallas_call(
        functools.partial(bwd_kernel, len(got), nbr.shape[2], scale),
        out_shape=[sds((3, rows, some))] * n,
        in_specs=[SMEM] * 3 + [ANY] * (len(got) + 4),
        out_specs=[vm] * n,
        scratch_shapes=[
            pltpu.VMEM((n, 3, rows, some), BF),
            pltpu.VMEM((2, n * rows, some), BF),
            pltpu.VMEM((n, rows, some), BF),
            pltpu.VMEM((n * rows, some), F32),
            pltpu.VMEM((n * rows, some), F32),
            pltpu.VMEM((nbr.shape[2] * BLK, some), BF),
            pltpu.VMEM((nbr.shape[2] * BLK, some), BF),
            pltpu.SemaphoreType.DMA((n + 2,)),
            pltpu.SemaphoreType.DMA((5,)),
        ],
        compiler_params=params(64),
        cost_estimate=COST,
        name="attend_back",
    )(me, nbr, cnt, *got, *terms)


def project_own_kernel(a_ref, w_ref, o_ref):
    o_ref[...] = dot(a_ref[...], w_ref[...])


def project_own(a, w, tile=512):
    rows, depth = a.shape
    cols = w.shape[1]
    return pl.pallas_call(
        project_own_kernel,
        grid=(cols // tile,),
        out_shape=sds((rows, cols), F32),
        in_specs=[
            pl.BlockSpec((rows, depth), lambda j: (0, 0)),
            pl.BlockSpec((depth, tile), lambda j: (0, j)),
        ],
        out_specs=pl.BlockSpec((rows, tile), lambda j: (0, j)),
        compiler_params=params(64),
        cost_estimate=COST,
        name="project_own",
    )(a, w)


def project_kernel(own_ref, b_ref, w_ref, *rest):
    y = own_ref[...] + dot(b_ref[...], w_ref[...])
    if len(rest) == 1:
        rest[0][...] = y.astype(BF)
        return
    far_ref, own_out, pair_out = rest
    y = (y + far_ref[...].astype(F32)).astype(BF)
    rows = own_out.shape[0]
    own_out[...] = y[:rows]
    pair_out[...] = y[rows:]


def project(own, b, w, begin, end, far=None, tile=512):
    rows, depth = b.shape
    rows //= 2
    cols = end - begin
    skip = begin // tile
    near = far is not None
    half = 0 if near else 1
    out = rows // 2 if near else rows
    return pl.pallas_call(
        project_kernel,
        grid=(cols // tile,),
        out_shape=[sds((out, cols))] * (2 if near else 1),
        in_specs=[
            pl.BlockSpec((rows, tile), lambda j: (half, skip + j)),
            pl.BlockSpec((rows, depth), lambda j: (half, 0)),
            pl.BlockSpec((depth, tile), lambda j: (0, skip + j)),
        ]
        + [pl.BlockSpec((rows, tile), lambda j: (0, j))] * int(near),
        out_specs=[pl.BlockSpec((out, tile), lambda j: (0, j))] * (2 if near else 1),
        compiler_params=params(64),
        cost_estimate=LONG if near else COST,
        name="project",
    )(own, b, w, *([far] if near else []))


def project_back_kernel(n, m, order, *refs):
    d_refs, w_refs, o_refs = refs[:n], refs[n : n + m], refs[n + m : n + 2 * m]
    held_d, held_w, sem = refs[n + 2 * m :]
    rows = d_refs[0].shape[0]
    copies = [
        pltpu.make_async_copy(d, held_d.at[pl.ds(i * rows, rows)], sem.at[i])
        for i, d in enumerate(d_refs)
    ] + [pltpu.make_async_copy(w, held_w.at[i], sem.at[n + i]) for i, w in enumerate(w_refs)]
    for c in copies:
        c.start()
    for c in copies[: n + 1]:
        c.wait()
    for i in range(m):
        if i:
            copies[n + i].wait()
        out = dot(held_d[...], held_w[i], NT).astype(BF)
        for r in range(n):
            there = order[i][r]
            o_refs[i][there * rows : (there + 1) * rows] = out[r * rows : (r + 1) * rows]


def project_back(ds, ws, order):
    n, m = len(ds), len(ws)
    rows, cols = ds[0].shape
    width = ws[0].shape[0]
    vm = pl.BlockSpec(memory_space=pltpu.VMEM)
    return pl.pallas_call(
        functools.partial(project_back_kernel, n, m, order),
        out_shape=[sds((n * rows, width))] * m,
        in_specs=[ANY] * (n + m),
        out_specs=[vm] * m,
        scratch_shapes=[
            pltpu.VMEM((n * rows, cols), BF),
            pltpu.VMEM((m, width, cols), BF),
            pltpu.SemaphoreType.DMA((n + m,)),
        ],
        compiler_params=params(64),
        cost_estimate=COST,
        name="project_back",
    )(*ds, *ws)


def weight_own_kernel(n, at, *refs):
    ds, o_ref, d = refs[:n], refs[n], refs[n + 1]
    rows = ds[0].shape[0]
    for r, piece in enumerate(ds):
        d[r * rows : (r + 1) * rows] = piece[...]
    o_ref[...] = dot(at[...], d[...])


def weight_own(at, ds, tile=512):
    n = len(ds)
    width = at.shape[0]
    rows, cols = ds[0].shape
    return pl.pallas_call(
        functools.partial(weight_own_kernel, n),
        grid=(cols // tile,),
        out_shape=sds((width, cols), F32),
        in_specs=[pl.BlockSpec((width, n * rows), lambda j: (0, 0))]
        + [pl.BlockSpec((rows, tile), lambda j: (0, j))] * n,
        out_specs=pl.BlockSpec((width, tile), lambda j: (0, j)),
        scratch_shapes=[pltpu.VMEM((n * rows, tile), BF)],
        compiler_params=params(64),
        cost_estimate=COST,
        name="weight_own",
    )(at, *ds)


def weight_kernel(n, done_ref, at, b_ref, *refs):
    ds, o_ref, bt, d = refs[:n], refs[n], refs[n + 1], refs[n + 2]
    rows = ds[0].shape[0]

    @pl.when(pl.program_id(0) == 0)
    def _():
        bt[...] = b_ref[...].T

    for r, piece in enumerate(ds):
        d[r * rows : (r + 1) * rows] = piece[...]
    own = done_ref[...] + dot(at[...], ds[n - 1][...])
    for i, out in enumerate((own, dot(bt[...], d[...]))):
        o_ref[:, i] = out.astype(BF).reshape(o_ref.shape[0], *o_ref.shape[2:])


def weight_grad(done, at, b, ds, owners, tile=1280):
    n = len(ds)
    tokens, width = b.shape
    rows, cols = ds[0].shape
    some = width // owners
    apart = owners if some % 16 == 0 else 1
    out = pl.pallas_call(
        functools.partial(weight_kernel, n),
        grid=(cols // tile,),
        out_shape=sds((apart, 2, width // apart, cols)),
        in_specs=[
            pl.BlockSpec((width, tile), lambda j: (0, j)),
            pl.BlockSpec((width, rows), lambda j: (0, n - 1)),
            pl.BlockSpec((tokens, width), lambda j: (0, 0)),
        ]
        + [pl.BlockSpec((rows, tile), lambda j: (0, j))] * n,
        out_specs=pl.BlockSpec((apart, 2, width // apart, tile), lambda j: (0, 0, 0, j)),
        scratch_shapes=[pltpu.VMEM((width, tokens), BF), pltpu.VMEM((tokens, tile), BF)],
        compiler_params=params(64),
        cost_estimate=COST,
        name="weight_grad",
    )(done, at, b, *ds)
    if apart == 1:
        out = out.reshape(2, owners, some, cols).swapaxes(0, 1)
    return out.reshape(2 * width, cols)


def on_device(n, owners, q_proj, k_proj, v_proj, neighbours, counts, w_out, d_out):
    scale = 1.0 / math.sqrt(HD)
    seq = lax.axis_index("seq")
    me = seq.astype(jnp.int32)[None]
    half = d_out.shape[2] // 2
    low = seq & 1

    def to(x, r):
        return lax.ppermute(x, "seq", [(i, i ^ r) for i in range(n)])

    def mine(x):
        return lax.dynamic_slice_in_dim(x, low * half, half, 1)

    def theirs(x):
        return lax.dynamic_slice_in_dim(x, (1 - low) * half, half, 1)

    def after(x, *others):
        return lax.optimization_barrier((x, *others))[0]

    sent = pack(me, q_proj, k_proj, v_proj, n)
    parts = [to(x, r) for r, x in enumerate(sent, 1)]
    got = [q_proj, k_proj, v_proj, *parts]
    sent = sent[0]

    w_out = after(w_out, sent)
    w_a = lax.all_gather(mine(w_out), "zero", axis=0, tiled=True)
    d_local = after(d_out, sent)[0]
    d0, d_theirs = mine(d_local), theirs(d_local)

    w_pair = after(to(theirs(after(w_out, d0, d_theirs)), 1), w_a, *parts)
    w_b = lax.all_gather(w_pair, "zero", axis=0, tiled=True)

    d1 = to(d_theirs, 1)
    d2 = to(d0, 2)

    attn, swapped, attn_t = attend(me, neighbours, counts, got, scale)
    attn_pair = to(swapped, 1)
    y_own = project_own(after(attn, swapped), w_a)
    d3 = to(after(d1, y_own), 2)

    (own_0,) = project_back([d0, d1, d2], [w_a], ((0, 1, 2),))
    (sent_0,) = project_back([d0, after(d1, own_0), d2], [w_b], ((1, 0, 2),))
    pair_0 = to(sent_0, 1)
    gw_own = weight_own(after(attn_t, sent_0), [d0, d1, d2])
    attn_pair = after(attn_pair, gw_own)

    near_cut = half * 2 // 5
    ranges = [(0, near_cut), (near_cut, half)]
    far_0 = project(y_own, attn_pair, w_b, *ranges[0])[0]
    (sent_1,) = project_back([after(d3, far_0)], [w_b], ((0,),))
    pair_1 = to(sent_1, 1)
    far_1 = project(y_own, after(attn_pair, sent_1), w_b, *ranges[1])[0]
    after_far = after(attn_pair, far_1)
    y_far = [to(far_0, 2), to(far_1, 2)]
    (own_1,) = project_back([after(d3, after_far)], [w_a], ((0,),))

    gw = weight_grad(gw_own, attn_t, after(after_far, own_1), [d0, d1, d2, d3], owners)

    terms = [own_0, after(own_1, gw), pair_0, pair_1]
    grads = attend_back(me, neighbours, counts, got, terms, scale)
    back = [grads[0]] + [to(x, r) for r, x in enumerate(grads[1:], 1)]

    ys, y_pair, last = [], [], gw
    for c, far in zip(ranges, y_far):
        ys.append(project(y_own, after(attn_pair, last), w_b, *c, far))
        y_pair.append(to(ys[-1][1], 1))
        last = y_pair[-1]
    out_y = join(low.astype(jnp.int32)[None], [y[0] for y in ys], y_pair)
    grad_q, grad_k, grad_v = unpack(me, [back])

    gw = lax.psum_scatter(after(gw, y_far[0], pair_0, pair_1), "zero", scatter_dimension=0, tiled=True)
    gw = after(gw, grads[0])
    rows = gw.shape[0] // 2
    gw_own, gw_pair = gw[:rows], to(gw[rows:], 1)
    grad_w = jnp.where(
        low == 0,
        jnp.concatenate([gw_own, gw_pair], axis=1),
        jnp.concatenate([gw_pair, gw_own], axis=1),
    ).astype(F32)
    return (out_y, grad_q, grad_k, grad_v, grad_w)


def solution(mesh):
    return jax.shard_map(
        functools.partial(on_device, mesh.shape["seq"], mesh.shape["zero"]),
        mesh=mesh,
        in_specs=(
            P("zero", "seq", None),
            P("zero", "seq", None),
            P("zero", "seq", None),
            P("zero", None, None),
            P("zero", None),
            P(("seq", "zero"), None),
            P("zero", "seq", None),
        ),
        out_specs=(
            P("zero", "seq", None),
            P("zero", "seq", None),
            P("zero", "seq", None),
            P("zero", "seq", None),
            P(("seq", "zero"), None),
        ),
        check_vma=False,
    )
```

```python
import functools
import math

import jax
import jax.numpy as jnp
from jax import lax
from jax.experimental import pallas as pl
from jax.experimental.pallas import tpu as pltpu
from jax.sharding import PartitionSpec as P

HD = 128
BLK = 128
MB = 1 << 20
BF = jnp.bfloat16
COST = pl.CostEstimate(flops=1024, bytes_accessed=1024, transcendentals=0)
LONG = pl.CostEstimate(flops=1024, bytes_accessed=1024, transcendentals=0)
F32 = jnp.float32


ANY = pl.BlockSpec(memory_space=pl.ANY)
SMEM = pl.BlockSpec(memory_space=pltpu.SMEM)


def params(mb):
    return pltpu.CompilerParams(vmem_limit_bytes=mb * MB)


def sds(shape, dtype=BF):
    return jax.ShapeDtypeStruct(shape, dtype)


def run_copies(copies):
    for c in copies:
        c.start()
    for c in copies:
        c.wait()


def staged(moves, *rest):
    held, sem_in, sem_out = rest[:-2], rest[-2], rest[-1]
    ins = [pltpu.make_async_copy(a, h, sem_in.at[i]) for i, ((a, _), h) in enumerate(zip(moves, held))]
    outs = [pltpu.make_async_copy(h, b, sem_out.at[i]) for i, ((_, b), h) in enumerate(zip(moves, held))]
    for c in ins:
        c.start()
    for c, o in zip(ins, outs):
        c.wait()
        o.start()
    for o in outs:
        o.wait()


def pack_kernel(n, width, me_ref, q_ref, k_ref, v_ref, w_ref, *rest):
    outs = rest[: n + 1]
    half = w_ref.shape[1] // 2
    moves = []
    for r, out in enumerate(outs[: n - 1], 1):
        col = pl.multiple_of((me_ref[0] ^ r) * width, 128)
        for t, src in enumerate((q_ref, k_ref, v_ref)):
            moves.append((src.at[0, :, pl.ds(col, width)], out.at[t]))
    for i, out in enumerate(outs[n - 1 :]):
        col = pl.multiple_of(((me_ref[0] & 1) ^ i) * half, 128)
        moves.append((w_ref.at[:, pl.ds(col, half)], out))
    staged(moves, *rest[n + 1 :])


def pack(me, q, k, v, w, n):
    rows, cols = q.shape[1:]
    width = cols // n
    w_half = (w.shape[0], w.shape[1] // 2)
    return pl.pallas_call(
        functools.partial(pack_kernel, n, width),
        out_shape=[sds((3, rows, width))] * (n - 1) + [sds(w_half)] * 2,
        in_specs=[SMEM, ANY, ANY, ANY, ANY],
        out_specs=[ANY] * (n + 1),
        scratch_shapes=[pltpu.VMEM((rows, width), BF)] * (3 * (n - 1))
        + [pltpu.VMEM(w_half, BF)] * 2
        + [pltpu.SemaphoreType.DMA((3 * n - 1,))] * 2,
        compiler_params=params(64),
        cost_estimate=COST,
        name="pack",
    )(me, q, k, v, w)


def load_copies(me, own, parts, held, sem):
    width = held.shape[3]
    col = pl.multiple_of(me * width, 128)
    copies = [
        pltpu.make_async_copy(x.at[0, :, pl.ds(col, width)], held.at[me, t], sem.at[t])
        for t, x in enumerate(own)
    ]
    for r, part in enumerate(parts, 1):
        copies.append(pltpu.make_async_copy(part, held.at[me ^ r], sem.at[2 + r]))
    return copies


def unpack_kernel(n, width, cuts, me_ref, *rest):
    m = n * len(cuts)
    parts, outs = rest[:m], rest[m : m + 3]
    moves = []
    for i, part in enumerate(parts):
        col = pl.multiple_of((me_ref[0] ^ (i % n)) * width + cuts[i // n], 128)
        for t in range(3):
            moves.append((part.at[t], outs[t].at[0, :, pl.ds(col, part.shape[2])]))
    staged(moves, *rest[m + 3 :])


def unpack(me, chunks):
    n = len(chunks[0])
    cuts = [sum(c[0].shape[2] for c in chunks[:i]) for i in range(len(chunks))]
    width = sum(c[0].shape[2] for c in chunks)
    rows = chunks[0][0].shape[1]
    parts = [x for c in chunks for x in c]
    return pl.pallas_call(
        functools.partial(unpack_kernel, n, width, cuts),
        out_shape=[sds((1, rows, n * width))] * 3,
        in_specs=[SMEM] + [ANY] * len(parts),
        out_specs=[ANY] * 3,
        scratch_shapes=[pltpu.VMEM(x.shape[1:], BF) for x in parts for _ in range(3)]
        + [pltpu.SemaphoreType.DMA((3 * len(parts),))] * 2,
        compiler_params=params(64),
        cost_estimate=LONG,
        name="unpack",
    )(me, *parts)


def join_kernel(width, low_ref, *rest):
    m = (len(rest) - 3) // 2
    parts, out = rest[:m], rest[m]
    moves, col = [], 0
    for i, part in enumerate(parts):
        if i == m // 2:
            col = 0
        side = low_ref[0] if i < m // 2 else 1 - low_ref[0]
        start = pl.multiple_of(side * width + col, 128)
        col += part.shape[1]
        moves.append((part, out.at[0, :, pl.ds(start, part.shape[1])]))
    staged(moves, *rest[m + 1 :])


def join(low, own, pair):
    parts = own + pair
    rows = parts[0].shape[0]
    width = sum(x.shape[1] for x in own)
    return pl.pallas_call(
        functools.partial(join_kernel, width),
        out_shape=sds((1, rows, 2 * width)),
        in_specs=[SMEM] + [ANY] * len(parts),
        out_specs=ANY,
        scratch_shapes=[pltpu.VMEM(x.shape, BF) for x in parts]
        + [pltpu.SemaphoreType.DMA((len(parts),))] * 2,
        compiler_params=params(64),
        cost_estimate=LONG,
        name="join",
    )(low, *parts)


def place(block, me, per):
    return pl.multiple_of((((block // per) ^ me) * per + block % per) * BLK, BLK)


NT = (((1,), (1,)), ((), ()))
TN = (((0,), (0,)), ((), ()))


def dot(a, b, dims=(((1,), (0,)), ((), ()))):
    return lax.dot_general(a, b, dims, preferred_element_type=F32)


def soft_of(scores, axis):
    expo = jnp.exp(scores - jnp.max(scores, axis=axis, keepdims=True))
    return expo * (1.0 / jnp.sum(expo, axis=axis, keepdims=True))


def for_blocks(blocks, slots, nbr_ref, cnt_ref, body):
    def block(b, _):
        for count in range(1, slots + 1):

            @pl.when(cnt_ref[0, b] == count)
            def _():
                body(b, [nbr_ref[0, b, j] for j in range(count)])

        return 0

    lax.fori_loop(0, blocks, block, 0)


def gather(held, t, keys, per, out):
    for j, e in enumerate(keys):
        rows = pl.ds(pl.multiple_of(e % per * BLK, BLK), BLK)
        out[j * BLK : (j + 1) * BLK] = held[e // per, t, rows]


def fwd_kernel(heads, slots, scale, me_ref, nbr_ref, cnt_ref, *rest):
    own, parts, (attn_ref, swap_ref, t_ref, held, ks, vs, sem) = rest[:3], rest[3:-7], rest[-7:]
    me = me_ref[0]
    run_copies(load_copies(me, own, parts, held, sem))
    n, per = held.shape[0], held.shape[2] // BLK

    def body(b, keys):
        here, there = place(b, me, per), place(b, me ^ 1, per)
        rows = pl.ds(pl.multiple_of(b % per * BLK, BLK), BLK)
        gather(held, 1, keys, per, ks)
        gather(held, 2, keys, per, vs)
        used = slice(0, len(keys) * BLK)
        cols = [slice(h * HD, (h + 1) * HD) for h in range(heads)]
        scores = [dot(held[b // per, 0, rows, c], ks[used, c], NT) * scale for c in cols]
        probs = [soft_of(x, 1).astype(BF) for x in scores]
        for c, p in zip(cols, probs):
            out = dot(p, vs[used, c]).astype(BF)
            attn_ref[pl.ds(here, BLK), c] = out
            swap_ref[pl.ds(there, BLK), c] = out

    for_blocks(n * per, slots, nbr_ref, cnt_ref, body)
    t_ref[...] = attn_ref[...].T


def attend(me, nbr, cnt, got, scale):
    n = len(got) - 2
    _, rows, width = got[3].shape
    vm = pl.BlockSpec(memory_space=pltpu.VMEM)
    return pl.pallas_call(
        functools.partial(fwd_kernel, width // HD, nbr.shape[2], scale),
        out_shape=[sds((n * rows, width))] * 2 + [sds((width, n * rows))],
        in_specs=[SMEM] * 3 + [ANY] * len(got),
        out_specs=[vm] * 3,
        scratch_shapes=[pltpu.VMEM((n, 3, rows, width), BF)]
        + [pltpu.VMEM((nbr.shape[2] * BLK, width), BF)] * 2
        + [pltpu.SemaphoreType.DMA((n + 2,))],
        compiler_params=params(64),
        cost_estimate=COST,
        name="attend",
    )(me, nbr, cnt, *got)


def bwd_kernel(n_got, slots, scale, me_ref, nbr_ref, cnt_ref, *rest):
    got, rest = rest[:n_got], rest[n_got:]
    d_refs, outs, (held, terms, dq, dk, dv, ks, vs, sem, d_sem) = rest[:4], rest[4:-9], rest[-9:]
    me = me_ref[0]
    n, _, rows, some = held.shape
    per = rows // BLK
    copies = load_copies(me, got[:3], got[3:], held, sem)
    own_0, own_1, pair_0, pair_1 = d_refs
    for i, (ref, begin, end, t, start) in enumerate(
        (
            (own_0, 0, 3, 0, 0),
            (own_1, 0, 1, 0, 3),
            (pair_0, 0, 2, 1, 0),
            (pair_0, 2, 3, 1, 3),
            (pair_1, 0, 1, 1, 2),
        )
    ):
        part, there = pl.ds(begin * rows, (end - begin) * rows), pl.ds(start * rows, (end - begin) * rows)
        copies.append(
            pltpu.make_async_copy(ref.at[part], terms.at[t, there], d_sem.at[i])
        )
    for c in copies:
        c.start()
    dk[...] = jnp.zeros_like(dk)
    dv[...] = jnp.zeros_like(dv)
    for c in copies:
        c.wait()

    def body(b, keys):
        here = pl.ds(place(b, me, per), BLK)
        rows_b = pl.ds(pl.multiple_of(b % per * BLK, BLK), BLK)
        gather(held, 1, keys, per, ks)
        gather(held, 2, keys, per, vs)
        used = slice(0, len(keys) * BLK)
        heads = [slice(h * HD, (h + 1) * HD) for h in range(some // HD)]
        qs = [held[b // per, 0, rows_b, c] for c in heads]
        ds = [
            (terms[0, here, c].astype(F32) + terms[1, here, c].astype(F32)).astype(BF)
            for c in heads
        ]
        softs = [soft_of(dot(ks[used, c], q, NT) * scale, 0) for c, q in zip(heads, qs)]
        dps = [dot(vs[used, c], d, NT) for c, d in zip(heads, ds)]
        dss = [
            (s * (p - jnp.sum(s * p, axis=0, keepdims=True))).astype(BF)
            for s, p in zip(softs, dps)
        ]
        for c, q, d, s, x in zip(heads, qs, ds, softs, dss):
            dq[b // per, rows_b, c] = (dot(x, ks[used, c], TN) * scale).astype(BF)
            to_v, to_k = dot(s.astype(BF), d), dot(x, q)
            for j, e in enumerate(keys):
                rows_e = pl.ds(pl.multiple_of(e * BLK, BLK), BLK)
                dv[rows_e, c] += to_v[j * BLK : (j + 1) * BLK]
                dk[rows_e, c] += to_k[j * BLK : (j + 1) * BLK]

    for_blocks(n * per, slots, nbr_ref, cnt_ref, body)
    for r, out in enumerate(outs):
        g = me ^ r
        rows_g = pl.ds(pl.multiple_of(g * rows, BLK), rows)
        out[0] = dq[g]
        out[1] = (dk[rows_g] * scale).astype(BF)
        out[2] = dv[rows_g].astype(BF)


def attend_back(me, nbr, cnt, got, terms, scale):
    n = len(got) - 2
    _, rows, some = got[3].shape
    vm = pl.BlockSpec(memory_space=pltpu.VMEM)
    return pl.pallas_call(
        functools.partial(bwd_kernel, len(got), nbr.shape[2], scale),
        out_shape=[sds((3, rows, some))] * n,
        in_specs=[SMEM] * 3 + [ANY] * (len(got) + 4),
        out_specs=[vm] * n,
        scratch_shapes=[
            pltpu.VMEM((n, 3, rows, some), BF),
            pltpu.VMEM((2, n * rows, some), BF),
            pltpu.VMEM((n, rows, some), BF),
            pltpu.VMEM((n * rows, some), F32),
            pltpu.VMEM((n * rows, some), F32),
            pltpu.VMEM((nbr.shape[2] * BLK, some), BF),
            pltpu.VMEM((nbr.shape[2] * BLK, some), BF),
            pltpu.SemaphoreType.DMA((n + 2,)),
            pltpu.SemaphoreType.DMA((5,)),
        ],
        compiler_params=params(64),
        cost_estimate=COST,
        name="attend_back",
    )(me, nbr, cnt, *got, *terms)


def project_own_kernel(a_ref, w_ref, o_ref):
    o_ref[...] = dot(a_ref[...], w_ref[...])


def project_own(a, w, tile=512):
    rows, depth = a.shape
    cols = w.shape[1]
    return pl.pallas_call(
        project_own_kernel,
        grid=(cols // tile,),
        out_shape=sds((rows, cols), F32),
        in_specs=[
            pl.BlockSpec((rows, depth), lambda j: (0, 0)),
            pl.BlockSpec((depth, tile), lambda j: (0, j)),
        ],
        out_specs=pl.BlockSpec((rows, tile), lambda j: (0, j)),
        compiler_params=params(64),
        cost_estimate=COST,
        name="project_own",
    )(a, w)


def project_kernel(own_ref, b_ref, w_ref, *rest):
    y = own_ref[...] + dot(b_ref[...], w_ref[...])
    if len(rest) == 1:
        rest[0][...] = y.astype(BF)
        return
    far_ref, own_out, pair_out = rest
    y = (y + far_ref[...].astype(F32)).astype(BF)
    rows = own_out.shape[0]
    own_out[...] = y[:rows]
    pair_out[...] = y[rows:]


def project(own, b, w, begin, end, far=None, tile=512):
    rows, depth = b.shape
    rows //= 2
    cols = end - begin
    skip = begin // tile
    near = far is not None
    half = 0 if near else 1
    out = rows // 2 if near else rows
    return pl.pallas_call(
        project_kernel,
        grid=(cols // tile,),
        out_shape=[sds((out, cols))] * (2 if near else 1),
        in_specs=[
            pl.BlockSpec((rows, tile), lambda j: (half, skip + j)),
            pl.BlockSpec((rows, depth), lambda j: (half, 0)),
            pl.BlockSpec((depth, tile), lambda j: (0, skip + j)),
        ]
        + [pl.BlockSpec((rows, tile), lambda j: (0, j))] * int(near),
        out_specs=[pl.BlockSpec((out, tile), lambda j: (0, j))] * (2 if near else 1),
        compiler_params=params(64),
        cost_estimate=LONG if near else COST,
        name="project",
    )(own, b, w, *([far] if near else []))


def project_back_kernel(n, m, order, *refs):
    d_refs, w_refs, o_refs = refs[:n], refs[n : n + m], refs[n + m : n + 2 * m]
    held_d, held_w, sem = refs[n + 2 * m :]
    rows = d_refs[0].shape[0]
    copies = [
        pltpu.make_async_copy(d, held_d.at[pl.ds(i * rows, rows)], sem.at[i])
        for i, d in enumerate(d_refs)
    ] + [pltpu.make_async_copy(w, held_w.at[i], sem.at[n + i]) for i, w in enumerate(w_refs)]
    for c in copies:
        c.start()
    for c in copies[: n + 1]:
        c.wait()
    for i in range(m):
        if i:
            copies[n + i].wait()
        out = dot(held_d[...], held_w[i], NT).astype(BF)
        for r in range(n):
            there = order[i][r]
            o_refs[i][there * rows : (there + 1) * rows] = out[r * rows : (r + 1) * rows]


def project_back(ds, ws, order):
    n, m = len(ds), len(ws)
    rows, cols = ds[0].shape
    width = ws[0].shape[0]
    vm = pl.BlockSpec(memory_space=pltpu.VMEM)
    return pl.pallas_call(
        functools.partial(project_back_kernel, n, m, order),
        out_shape=[sds((n * rows, width))] * m,
        in_specs=[ANY] * (n + m),
        out_specs=[vm] * m,
        scratch_shapes=[
            pltpu.VMEM((n * rows, cols), BF),
            pltpu.VMEM((m, width, cols), BF),
            pltpu.SemaphoreType.DMA((n + m,)),
        ],
        compiler_params=params(64),
        cost_estimate=COST,
        name="project_back",
    )(*ds, *ws)


def weight_own_kernel(n, at, *refs):
    ds, o_ref, d = refs[:n], refs[n], refs[n + 1]
    rows = ds[0].shape[0]
    for r, piece in enumerate(ds):
        d[r * rows : (r + 1) * rows] = piece[...]
    o_ref[...] = dot(at[...], d[...])


def weight_own(at, ds, tile=512):
    n = len(ds)
    width = at.shape[0]
    rows, cols = ds[0].shape
    return pl.pallas_call(
        functools.partial(weight_own_kernel, n),
        grid=(cols // tile,),
        out_shape=sds((width, cols), F32),
        in_specs=[pl.BlockSpec((width, n * rows), lambda j: (0, 0))]
        + [pl.BlockSpec((rows, tile), lambda j: (0, j))] * n,
        out_specs=pl.BlockSpec((width, tile), lambda j: (0, j)),
        scratch_shapes=[pltpu.VMEM((n * rows, tile), BF)],
        compiler_params=params(64),
        cost_estimate=COST,
        name="weight_own",
    )(at, *ds)


def weight_kernel(n, done_ref, at, b_ref, *refs):
    ds, o_ref, bt, d = refs[:n], refs[n], refs[n + 1], refs[n + 2]
    rows = ds[0].shape[0]

    @pl.when(pl.program_id(0) == 0)
    def _():
        bt[...] = b_ref[...].T

    for r, piece in enumerate(ds):
        d[r * rows : (r + 1) * rows] = piece[...]
    own = done_ref[...] + dot(at[...], ds[n - 1][...])
    for i, out in enumerate((own, dot(bt[...], d[...]))):
        o_ref[:, i] = out.astype(BF).reshape(o_ref.shape[0], *o_ref.shape[2:])


def weight_grad(done, at, b, ds, owners, tile=1280):
    n = len(ds)
    tokens, width = b.shape
    rows, cols = ds[0].shape
    some = width // owners
    apart = owners if some % 16 == 0 else 1
    out = pl.pallas_call(
        functools.partial(weight_kernel, n),
        grid=(cols // tile,),
        out_shape=sds((apart, 2, width // apart, cols)),
        in_specs=[
            pl.BlockSpec((width, tile), lambda j: (0, j)),
            pl.BlockSpec((width, rows), lambda j: (0, n - 1)),
            pl.BlockSpec((tokens, width), lambda j: (0, 0)),
        ]
        + [pl.BlockSpec((rows, tile), lambda j: (0, j))] * n,
        out_specs=pl.BlockSpec((apart, 2, width // apart, tile), lambda j: (0, 0, 0, j)),
        scratch_shapes=[pltpu.VMEM((width, tokens), BF), pltpu.VMEM((tokens, tile), BF)],
        compiler_params=params(64),
        cost_estimate=COST,
        name="weight_grad",
    )(done, at, b, *ds)
    if apart == 1:
        out = out.reshape(2, owners, some, cols).swapaxes(0, 1)
    return out.reshape(2 * width, cols)


def on_device(n, owners, q_proj, k_proj, v_proj, neighbours, counts, w_out, d_out):
    scale = 1.0 / math.sqrt(HD)
    seq = lax.axis_index("seq")
    me = seq.astype(jnp.int32)[None]
    half = d_out.shape[2] // 2
    low = seq & 1

    def to(x, r):
        return lax.ppermute(x, "seq", [(i, i ^ r) for i in range(n)])

    def mine(x):
        return lax.dynamic_slice_in_dim(x, low * half, half, 1)

    def theirs(x):
        return lax.dynamic_slice_in_dim(x, (1 - low) * half, half, 1)

    def after(x, *others):
        return lax.optimization_barrier((x, *others))[0]

    *sent, w_mine, w_theirs = pack(me, q_proj, k_proj, v_proj, w_out, n)
    parts = [to(x, r) for r, x in enumerate(sent, 1)]
    got = [q_proj, k_proj, v_proj, *parts]
    sent = sent[0]

    w_a = lax.all_gather(w_mine, "zero", axis=0, tiled=True)
    d_local = after(d_out, sent)[0]
    d0, d_theirs = mine(d_local), theirs(d_local)

    w_pair = after(to(after(w_theirs, d0, d_theirs), 1), w_a, *parts)
    w_b = lax.all_gather(w_pair, "zero", axis=0, tiled=True)

    d1 = to(d_theirs, 1)
    d2 = to(d0, 2)

    attn, swapped, attn_t = attend(me, neighbours, counts, got, scale)
    attn_pair = to(swapped, 1)
    y_own = project_own(after(attn, swapped), w_a)
    d3 = to(after(d1, y_own), 2)

    (own_0,) = project_back([d0, d1, d2], [w_a], ((0, 1, 2),))
    (sent_0,) = project_back([d0, after(d1, own_0), d2], [w_b], ((1, 0, 2),))
    pair_0 = to(sent_0, 1)
    gw_own = weight_own(after(attn_t, sent_0), [d0, d1, d2])
    attn_pair = after(attn_pair, gw_own)

    near_cut = half * 2 // 5
    ranges = [(0, near_cut), (near_cut, half)]
    far_0 = project(y_own, attn_pair, w_b, *ranges[0])[0]
    (sent_1,) = project_back([after(d3, far_0)], [w_b], ((0,),))
    pair_1 = to(sent_1, 1)
    far_1 = project(y_own, after(attn_pair, sent_1), w_b, *ranges[1])[0]
    after_far = after(attn_pair, far_1)
    y_far = [to(far_0, 2), to(far_1, 2)]
    (own_1,) = project_back([after(d3, after_far)], [w_a], ((0,),))

    gw = weight_grad(gw_own, attn_t, after(after_far, own_1), [d0, d1, d2, d3], owners)

    terms = [own_0, after(own_1, gw), pair_0, pair_1]
    grads = attend_back(me, neighbours, counts, got, terms, scale)
    back = [grads[0]] + [to(x, r) for r, x in enumerate(grads[1:], 1)]

    ys, y_pair, last = [], [], gw
    for c, far in zip(ranges, y_far):
        ys.append(project(y_own, after(attn_pair, last), w_b, *c, far))
        y_pair.append(to(ys[-1][1], 1))
        last = y_pair[-1]
    out_y = join(low.astype(jnp.int32)[None], [y[0] for y in ys], y_pair)
    grad_q, grad_k, grad_v = unpack(me, [back])

    gw = lax.psum_scatter(after(gw, y_far[0], pair_0, pair_1), "zero", scatter_dimension=0, tiled=True)
    gw = after(gw, grads[0])
    rows = gw.shape[0] // 2
    gw_own, gw_pair = gw[:rows], to(gw[rows:], 1)
    grad_w = jnp.where(
        low == 0,
        jnp.concatenate([gw_own, gw_pair], axis=1),
        jnp.concatenate([gw_pair, gw_own], axis=1),
    ).astype(F32)
    return (out_y, grad_q, grad_k, grad_v, grad_w)


def solution(mesh):
    return jax.shard_map(
        functools.partial(on_device, mesh.shape["seq"], mesh.shape["zero"]),
        mesh=mesh,
        in_specs=(
            P("zero", "seq", None),
            P("zero", "seq", None),
            P("zero", "seq", None),
            P("zero", None, None),
            P("zero", None),
            P(("seq", "zero"), None),
            P("zero", "seq", None),
        ),
        out_specs=(
            P("zero", "seq", None),
            P("zero", "seq", None),
            P("zero", "seq", None),
            P("zero", "seq", None),
            P(("seq", "zero"), None),
        ),
        check_vma=False,
    )
```
